32 devices in a mesh: parts: 2 (over y), tm: 4 (over z), factor: 4 (over x, core).
Axes of the slice: x: 2, y: 2, z: 4, core: 2. Of those that a mesh axis runs over, the one named last changes fastest.
Arguments:
- schur_matrix: float32 [24576, 24, 4, 128], P(('parts', 'tm'), None, 'factor'), parts along dimension 0, as said below
- link_rhs: float32 [24576], P(('parts', 'tm')), parts along dimension 0, may hold values from -6 to 6
- hour_rhs: float32 [32, 256], P(('parts', 'tm', 'factor')), parts along dimension 0, may hold values from -6 to 6
- link_cols: int32 [32, 256], P(('parts', 'tm', 'factor')), parts along dimension 0, may hold values from 0 to 255
- link_coef: float32 [32, 256], P(('parts', 'tm', 'factor')), parts along dimension 0, may hold values from -6 to 6
- hour_inverse: float32 [32, 256, 256], P(('parts', 'tm', 'factor')), parts along dimension 0, may hold values from -0.375 to 0.375
- couple_prev: float32 [32, 2, 256], P(('parts', 'tm', 'factor')), parts along dimension 0, may hold values from -1.2 to 1.2
- couple_next: float32 [32, 2, 256], P(('parts', 'tm', 'factor')), parts along dimension 0, may hold values from -1.2 to 1.2
Outputs:
- schur_trail: float32 [24576, 24, 4, 128], P(('parts', 'tm'), None, 'factor'), parts along dimension 0
- link_trail: float32 [24576], P(('parts', 'tm')), parts along dimension 0
- hour_step: float32 [32, 256], P(('parts', 'tm', 'factor')), parts along dimension 0
The draws below stay inside these ranges and needn't reach their ends.
There are 2 independent parts, one for each index of `parts`. The reference program is written for one: setup_inputs(seed, part) draws one part's arguments, and reference() takes and returns one part's arrays. A program takes and returns all parts, laid end to end along the dimension named above; each array names one. Nothing has to cross between parts.
Inputs may be any that keep to these rules, and one draw needn't show every extreme that they name: schur_matrix is symmetric and its leading 2 * 128 rows and columns form a positive definite block.
All inputs are finite; a program needn't handle non-finite values.
Results may differ from the reference program's by a relative error of at most 0.0001.
Values sent between devices are 32-bit elements; how exact they have to be, the bound alone decides.
A program may use at most 192 MiB of HBM per device.

```python
import math
import jax
import jax.numpy as jnp
from jax import lax

L = 12288
P_SIZE = 128
PANELS = 2
HB = 256
BW = 2
SWEEPS = 2
HOURS = 16
N_FACTOR = 4


def draw_schur_matrix(key, part):
    first_key, second_key = jax.random.split(jax.random.fold_in(key, 11))
    noise = jax.random.uniform(first_key, (L, L), jnp.float32, -1.0, 1.0)
    offdiag = (noise + noise.T) * (1.0 / math.sqrt(L))
    diag_vals = jax.random.uniform(second_key, (L,), jnp.float32, 1.0, 3.0) + PANELS * P_SIZE * 2.0 / math.sqrt(L)
    eye_mat = jnp.eye(L, dtype=jnp.float32)
    whole = offdiag * (1.0 - eye_mat) + eye_mat * diag_vals[:, None]
    return whole.reshape(L, L // (P_SIZE * N_FACTOR), N_FACTOR, P_SIZE)


def set_ends(drawn, own_key, least, largest):
    longest = drawn.shape.index(max(drawn.shape))
    spots = []
    for shift in (0, 1):
        where = [jax.random.randint(jax.random.fold_in(own_key, axis), (), 0, length) for axis, length in enumerate(drawn.shape)]
        where[longest] = (where[longest] + shift) % drawn.shape[longest]
        spots.append(tuple(where))
    return drawn.at[spots[0]].set(least).at[spots[1]].set(largest)


def steps_of(rng, extent, cuts, low, top_value):
    level, own = 1.0, jax.random.fold_in(rng, 6)
    for position, shards_of in cuts:
        draws = jnp.exp(jax.random.uniform(jax.random.fold_in(own, position), (shards_of,), jnp.float32, low / len(cuts), top_value / len(cuts)))
        level = level * jnp.repeat(draws, extent[position] // shards_of).reshape([-1 if axis == position else 1 for axis in range(len(extent))])
    return level


def gaussian(rng, dims, deviation, most, cuts=(), kind=jnp.bfloat16):
    array = deviation * jax.random.normal(rng, dims, jnp.float32)
    if cuts:
        array = array * steps_of(rng, dims, cuts, -0.22, 0.18)
    return jnp.clip(array, -most, most).astype(kind)


def setup_inputs(seed: int = 0, part: int = 0) -> dict:
    seeds = jax.random.split(jax.random.key(seed), 9)
    part_keys = jax.random.split(jax.random.fold_in(seeds[8], part), 9)
    return {
        "schur_matrix": draw_schur_matrix(jax.random.fold_in(jax.random.fold_in(seeds[8], part), 71), part),
        "link_rhs": gaussian(part_keys[1], (L,), 1.0, 6.0, ((0, 4),), jnp.float32),
        "hour_rhs": gaussian(part_keys[2], (HOURS, HB), 1.0, 6.0, ((0, 16),), jnp.float32),
        "link_cols": set_ends(jax.random.randint(part_keys[3], (HOURS, HB), 0, PANELS * P_SIZE), jax.random.fold_in(part_keys[3], 1), 0, (PANELS * P_SIZE) - 1).astype(jnp.int32),
        "link_coef": gaussian(part_keys[4], (HOURS, HB), 1.0, 6.0, ((0, 16),), jnp.float32),
        "hour_inverse": gaussian(part_keys[5], (HOURS, HB, HB), HB ** -0.5, 0.375, ((0, 16),), jnp.float32),
        "couple_prev": gaussian(part_keys[6], (HOURS, BW, HB), 0.2, 1.2, ((0, 16),), jnp.float32),
        "couple_next": gaussian(part_keys[7], (HOURS, BW, HB), 0.2, 1.2, ((0, 16),), jnp.float32),
    }


def reference(schur_matrix, link_rhs, hour_rhs, link_cols, link_coef, hour_inverse, couple_prev, couple_next):
    schur_now = schur_matrix.reshape(L, L)
    rhs_now = link_rhs
    all_rows = jnp.arange(L, dtype=jnp.int32)
    solved = []
    for panel_id in range(PANELS):
        panel_first = panel_id * P_SIZE
        panel_cols = schur_now[:, panel_first:panel_first + P_SIZE]
        diag_block = panel_cols[panel_first:panel_first + P_SIZE]
        lower_block = jnp.linalg.cholesky(diag_block)
        factor_rows = jax.scipy.linalg.solve_triangular(lower_block, panel_cols.T, lower=True).T
        factor_rows = jnp.where((all_rows < panel_first)[:, None], jnp.zeros_like(factor_rows), factor_rows)
        link_step = jax.scipy.linalg.solve_triangular(lower_block, rhs_now[panel_first:panel_first + P_SIZE], lower=True)
        rhs_now = rhs_now - jnp.dot(factor_rows, link_step, precision=lax.Precision.HIGHEST)
        schur_now = schur_now - jnp.dot(factor_rows, factor_rows.T, precision=lax.Precision.HIGHEST)
        solved.append(link_step)
    link_values = jnp.concatenate(solved)
    one_hot = (link_cols[:, :, None] == jnp.arange(PANELS * P_SIZE, dtype=jnp.int32)[None, None, :]).astype(jnp.float32)
    looked = jnp.einsum('hik,k->hi', one_hot, link_values, precision=lax.Precision.HIGHEST)
    target = hour_rhs - link_coef * looked
    hour_state = jnp.einsum('hik,hk->hi', hour_inverse, target, precision=lax.Precision.HIGHEST)
    for sweep_id in range(SWEEPS):
        zero_rows = jnp.zeros((1, BW), jnp.float32)
        prev_last = jnp.concatenate((zero_rows, hour_state[:-1, -BW:]), axis=0)
        next_first = jnp.concatenate((hour_state[1:, :BW], zero_rows), axis=0)
        coupling = jnp.einsum('hbi,hb->hi', couple_prev, prev_last, precision=lax.Precision.HIGHEST)
        coupling = coupling + jnp.einsum('hbi,hb->hi', couple_next, next_first, precision=lax.Precision.HIGHEST)
        hour_state = jnp.einsum('hik,hk->hi', hour_inverse, target - coupling, precision=lax.Precision.HIGHEST)
    return (schur_now.reshape(schur_matrix.shape), rhs_now, hour_state)
```

```python
import functools

import jax
import jax.numpy as jnp
from jax import lax
from jax.experimental import pallas as pl
from jax.experimental.pallas import tpu as pltpu
from jax.sharding import PartitionSpec as P

PANELS = 2
BW = 2
SWEEPS = 2
HIGH = lax.Precision.HIGHEST
MESH = pl.DeviceIdType.MESH


def spread(array, axis, root):
    mine = lax.axis_index(axis) == root
    return lax.psum(jnp.where(mine, array, jnp.zeros_like(array)), axis)


def with_halo(cells, sides, width):
    for axis, dim in sides:
        count = lax.axis_size(axis)
        ends = count - 1
        head = lax.slice_in_dim(cells, 0, width, axis=dim)
        tail = lax.slice_in_dim(cells, cells.shape[dim] - width, cells.shape[dim], axis=dim)
        cells = jnp.concatenate(
            [
                lax.ppermute(tail, axis, [(i, (i + 1) % count) for i in range(ends)]),
                cells,
                lax.ppermute(head, axis, [((i + 1) % count, i) for i in range(ends)]),
            ],
            axis=dim,
        )
    return cells


W = 128
NZ = 4
EARLY = 4


def across(a, b):
    return lax.dot_general(
        a, b, (((1,), (1,)), ((), ())), precision=HIGH, preferred_element_type=jnp.float32)


def matmul(a, b):
    return jnp.dot(a, b, precision=HIGH, preferred_element_type=jnp.float32)


def split(a):
    high = a.astype(jnp.bfloat16)
    return high, (a - high.astype(jnp.float32)).astype(jnp.bfloat16)


def chol_inverse(block, hooks):
    count = W // 8
    rows = [block[8 * i:8 * i + 8, :] for i in range(count)]
    lane = lax.broadcasted_iota(jnp.int32, (8, W), 1)
    sub = lax.broadcasted_iota(jnp.int32, (8, W), 0)
    for b in range(count):
        j0 = 8 * b
        here = (lane >= j0) & (lane < j0 + 8)
        p = rows[b]
        piv = [jnp.broadcast_to(p[:, j0 + t:j0 + t + 1], (8, W)) for t in range(8)]
        p = jnp.where(here, jnp.where(lane - j0 == sub, 1.0, 0.0), p)
        done = p
        for t in range(8):
            d = piv[t][t:t + 1, :]
            r = p[t:t + 1, :]
            done = jnp.where(sub == t, r * lax.rsqrt(d), done)
            inv = 1.0 / d
            rr = r * inv
            p = jnp.where(sub == t, rr, p - piv[t] * rr)
            for u in range(t + 1, 8):
                bu = piv[u][t:t + 1, :] * inv
                piv[u] = jnp.where(sub == t, bu, piv[u] - piv[t] * bu)
        for i in range(b + 1, count):
            old = rows[i]
            now = jnp.where(here, 0.0, old)
            for t in range(8):
                now = now - old[:, j0 + t:j0 + t + 1] * p[t:t + 1, :]
            rows[i] = now
        rows[b] = done
        if b in hooks:
            hooks[b]()
    full = jnp.concatenate(rows, axis=0)
    low = lax.broadcasted_iota(jnp.int32, (W, W), 0) >= lax.broadcasted_iota(jnp.int32, (W, W), 1)
    return jnp.where(low, full, 0.0)


def product(left, right):
    high = left[:, :2 * W]
    rows = jnp.concatenate([high, high, left[:, 2 * W:]], axis=1)
    first = right[:2 * W, :]
    cols = jnp.concatenate([first, right[2 * W:, :], first], axis=0)
    return jnp.dot(rows, cols, preferred_element_type=jnp.float32)


def pair_update(s, left, g, q, j, pairs, blocks):
    right = g.at[q * pairs + j]
    for qq in range(NZ):
        @pl.when(q == qq)
        def _():
            def body(b, carry):
                at = pl.ds(pl.multiple_of(b * 2 * W, 2 * W), 2 * W)
                u = product(left[at, :], right[...])
                s[qq][2 * j, at, :] -= u[:, :W]
                s[qq][2 * j + 1, at, :] -= u[:, W:]
                return carry
            lax.fori_loop(0, blocks, body, 0)


def panel_kernel(
    nc, s_hbm, rhs, h_rhs, h_cols, h_coef, h_inv, c_prev, c_next,
    s0, s1, s2, s3, left, g, trail, hour,
    cr, cc, dp, rs, hx, hl, inv_ref,
    lsem, ssem, osem, xs, xr, ms, mr, fs, fr, bs, br, dzs, dzr, dxs, dxr, dms, dmr, rss, rsr, hs, hr,
):
    s = (s0, s1, s2, s3)
    f = lax.axis_index("factor")
    z = lax.axis_index("tm")
    p = lax.rem(f, 2)
    q = 1 - p
    xx = lax.div(f, 2)
    mate = {"factor": f + 1 - 2 * p}
    over = {"factor": f + 2 - 4 * xx}
    blocks = 2 * nc
    pairs = nc // 2

    def remote(src, dst, send, recv, device):
        return pltpu.make_async_remote_copy(
            src_ref=src, dst_ref=dst, send_sem=send, recv_sem=recv, device_id=device, device_id_type=MESH)

    def load(b):
        return pltpu.make_async_copy(
            s_hbm.at[b * 2 * W:(b + 1) * 2 * W, 0, 0, :], cr.at[p, b], lsem.at[b])

    def tile_in(t):
        return pltpu.make_async_copy(s_hbm.at[:, t, 0, :], s[t // nc].at[t % nc], ssem.at[t])

    def xcopy(b):
        return remote(cr.at[p, b], cr.at[p, b], xs.at[b], xr.at[b], over)

    def mcopy(panel, b):
        return remote(cr.at[panel, b], cr.at[panel, b], ms.at[b], mr.at[b], mate)

    def slot(quarter, c):
        return cc.at[:, quarter, c // 2, (c % 2) * W:(c % 2 + 1) * W]

    def mine(c):
        return cr.at[:, 2 * c + xx, pl.ds(pl.multiple_of(p * W, W), W)]

    def own_copy(c):
        return pltpu.make_async_copy(mine(c), slot(z, c), osem.at[c])

    def fwd(m):
        c = m % nc
        where = slot(z - m // nc, c)
        return remote(mine(c) if m < nc else where, where, fs.at[m], fr.at[m], {"tm": z + 1})

    def bwd(m):
        c = m % nc
        where = slot(z + m // nc, c)
        return remote(mine(c) if m < nc else where, where, bs.at[m], br.at[m], {"tm": z - 1})

    def fwd_in(m):
        where = slot(z - 1 - m // nc, m % nc)
        return remote(where, where, fs.at[m], fr.at[m], {"tm": z - 1})

    def bwd_in(m):
        where = slot(z + 1 + m // nc, m % nc)
        return remote(where, where, bs.at[m], br.at[m], {"tm": z + 1})

    def own_sends(c):
        own_copy(c).start()

        @pl.when(z < NZ - 1)
        def _():
            fwd(c).start()

        @pl.when(z > 0)
        def _():
            bwd(c).start()

    def poll(m):
        if not 0 <= m < (NZ - 1) * nc:
            return
        step = m // nc

        @pl.when(z > step)
        def _():
            fwd_in(m).wait_recv()
            if step < NZ - 2:
                @pl.when(z < NZ - 1)
                def _():
                    fwd(m + nc).start()

        @pl.when(z < NZ - 1 - step)
        def _():
            bwd_in(m).wait_recv()
            if step < NZ - 2:
                @pl.when(z > 0)
                def _():
                    bwd(m + nc).start()

    def x1(c):
        @pl.when(xx == 1)
        def _():
            xcopy(2 * c + 1).wait_recv()
            mcopy(p, 2 * c + 1).start()
            mcopy(q, 2 * c + 1).wait_recv()
            own_sends(c)

    def x0(c):
        @pl.when(xx == 1)
        def _():
            xcopy(2 * c).wait_recv()
            mcopy(p, 2 * c).start()
            mcopy(q, 2 * c).wait_recv()

    def d_z(to):
        return remote(cr.at[p, 0], dp.at[p], dzs.at[to - 1], dzr, {"tm": to})

    def r_z(to):
        return remote(rhs.at[0:8], rs, rss.at[to - 1], rsr, {"tm": to})

    def d_x():
        return remote(dp.at[p], dp.at[p], dxs, dxr, over)

    def d_m(panel):
        return remote(dp.at[panel], dp.at[panel], dms, dmr, mate)

    has_prev = (z > 0) | (f > 0)
    has_next = (z < NZ - 1) | (f < 3)

    def h_prev(k):
        return remote(hx.at[k], hl.at[k, 1], hs.at[k, 0], hr.at[k, 1],
                      {"tm": jnp.where(f > 0, z, z - 1), "factor": jnp.where(f > 0, f - 1, 3)})

    def h_next(k):
        return remote(hx.at[k], hl.at[k, 0], hs.at[k, 1], hr.at[k, 0],
                      {"tm": jnp.where(f < 3, z, z + 1), "factor": jnp.where(f < 3, f + 1, 0)})

    @pl.when(xx == 0)
    def _():
        for b in range(blocks):
            load(b).start()

    for t in range(NZ * nc):
        tile_in(t).start()
    hl[...] = jnp.zeros_like(hl)

    barrier = pltpu.get_barrier_semaphore()

    def greet(device):
        pl.semaphore_signal(barrier, inc=1, device_id=device, device_id_type=MESH)

    greet(mate)
    greet(over)
    for step in range(1, NZ):
        greet({"tm": lax.rem(z + step, NZ)})
    middle = (f == 1) | (f == 2)
    up = (f == 3) & (z < NZ - 1)
    down = (f == 0) & (z > 0)

    @pl.when(middle)
    def _():
        greet({"factor": 3 - f})

    @pl.when(up)
    def _():
        greet({"tm": z + 1, "factor": 0})

    @pl.when(down)
    def _():
        greet({"tm": z - 1, "factor": 3})

    pl.semaphore_wait(barrier, NZ + 1 + jnp.where(middle | up | down, 1, 0))

    @pl.when(z == 0)
    def _():
        for to in range(1, NZ):
            r_z(to).start()
        rs[...] = rhs[0:8, :]

    @pl.when(xx == 0)
    def _():
        load(0).wait()

        @pl.when(z == 0)
        def _():
            for to in range(NZ - 1, 0, -1):
                d_z(to).start()
            dp[p] = cr[p, 0]
            d_x().start()
            d_m(p).start()

        for c in range(nc):
            if c > 0:
                load(2 * c).wait()
            load(2 * c + 1).wait()
            xcopy(2 * c + 1).start()
            mcopy(p, 2 * c).start()
            mcopy(p, 2 * c + 1).start()
        for c in range(nc):
            mcopy(q, 2 * c).wait_recv()
            mcopy(q, 2 * c + 1).wait_recv()
            own_sends(c)

    x1(0)
    x1(1)

    @pl.when((xx == 0) & (z > 0))
    def _():
        d_z(1).wait_recv()
        d_x().start()
        d_m(p).start()

    @pl.when(xx == 1)
    def _():
        d_x().wait_recv()
        d_m(p).start()

    d_m(q).wait_recv()

    def service(k):
        if k < nc:
            x1(k)
        poll(k - 2)

    top = chol_inverse(dp[0, 0:W, :], {4: lambda: service(2), 11: lambda: service(3)})

    @pl.when(xx == 0)
    def _():
        for c in range(nc):
            xcopy(2 * c).start()

    side = across(dp[0, W:, :], top)
    low = chol_inverse(
        dp[1, W:, :] - across(side, side), {0: lambda: service(4), 8: lambda: service(5)})
    mixed = -matmul(low, matmul(side, top))
    service(6)
    inv_ref[:W, :W] = top
    inv_ref[:W, W:] = jnp.zeros((W, W), jnp.float32)
    inv_ref[W:, :W] = mixed
    inv_ref[W:, W:] = low

    @pl.when(z > 0)
    def _():
        r_z(1).wait_recv()

    seg = jnp.concatenate([rs[0:1, :], rs[1:2, :]], axis=1)
    link = across(jnp.broadcast_to(seg, (8, 2 * W)), inv_ref[...])
    hot = (lax.broadcasted_iota(jnp.int32, (2 * W, 2 * W), 0) == h_cols[...]).astype(jnp.float32)
    target = h_rhs[...] - h_coef[...] * matmul(link, hot)

    def solve(k, want):
        hx[k] = across(want, h_inv[0])
        if k < SWEEPS:
            @pl.when(has_prev)
            def _():
                h_prev(k).start()

            @pl.when(has_next)
            def _():
                h_next(k).start()

    def sweep(k):
        @pl.when(has_prev)
        def _():
            h_next(k).wait_recv()

        @pl.when(has_next)
        def _():
            h_prev(k).wait_recv()

        before = hl[k, 0]
        after = hl[k, 1]
        coupling = before[:, 2 * W - 2:2 * W - 1] * c_prev[0, 0:1, :]
        coupling = coupling + before[:, 2 * W - 1:2 * W] * c_prev[0, 1:2, :]
        coupling = coupling + after[:, 0:1] * c_next[0, 0:1, :]
        coupling = coupling + after[:, 1:2] * c_next[0, 1:2, :]
        solve(k + 1, target - coupling)

    solve(0, target)

    def frow(b):
        fr_ = across(cr[0, b], inv_ref[:, :W]) + across(cr[1, b], inv_ref[:, W:])
        if not isinstance(b, int) or b == 0:
            row = lax.broadcasted_iota(jnp.int32, fr_.shape, 0) + (z * blocks + b) * 2 * W
            depth = lax.broadcasted_iota(jnp.int32, fr_.shape, 1)
            fr_ = jnp.where((row < W) & (depth >= W), 0.0, fr_)
        high, rest = split(fr_)
        at = pl.ds(b * 2 * W, 2 * W)
        left[at, :2 * W] = high
        left[at, 2 * W:] = rest
        gone = across(link, fr_)
        trail[pl.ds(2 * b, 1), :] = rhs[pl.ds(2 * b, 1), :] - gone[0:1, :W]
        trail[pl.ds(2 * b + 1, 1), :] = rhs[pl.ds(2 * b + 1, 1), :] - gone[0:1, W:]

    def fcol(quarter, j):
        gg = across(inv_ref[:, :W], cc[0, quarter, j]) + across(inv_ref[:, W:], cc[1, quarter, j])
        limit = jnp.where((quarter == 0) & (j == 0) & (f == 0), W, 0)
        depth = lax.broadcasted_iota(jnp.int32, gg.shape, 0)
        col = lax.broadcasted_iota(jnp.int32, gg.shape, 1)
        high, rest = split(jnp.where((depth >= W) & (col < limit), 0.0, gg))
        at = quarter * pairs + j
        g[at, :2 * W, :] = high
        g[at, 2 * W:, :] = rest

    def received(n, update):
        step, j = n // pairs, n % pairs

        @pl.when(z > step)
        def _():
            fcol(z - 1 - step, j)
            if update:
                pair_update(s, left, g, z - 1 - step, j, pairs, blocks)

        @pl.when(z < NZ - 1 - step)
        def _():
            fcol(z + 1 + step, j)
            if update:
                pair_update(s, left, g, z + 1 + step, j, pairs, blocks)

    for c in range(nc):
        frow(2 * c + 1)
        if c % 3 == 2:
            service(7 + c // 3)
    sweep(0)
    for c in range(nc):
        own_copy(c).wait()
    for c in range(nc):
        x0(c)
        service(9 + c)
        frow(2 * c)
        if c == nc // 2:
            sweep(1)
    hour[...] = hx[SWEEPS, 0:1, :]
    for t in range(NZ * nc):
        tile_in(t).wait()
    nxt = 9 + nc
    for j in range(pairs):
        fcol(z, j)
        pair_update(s, left, g, z, j, pairs, blocks)
        service(nxt + j)
    nxt += pairs
    total = (NZ - 1) * nc
    for n in range(total // 2):
        while nxt - 3 < 2 * n + 1:
            service(nxt)
            nxt += 1
        received(n, n < EARLY)
        if n < EARLY:
            service(nxt)
            nxt += 1

    for b in range(blocks):
        mcopy(p, b).wait_send()

        @pl.when(xx == 0)
        def _():
            xcopy(b).wait_send()

    for m in range(total):
        @pl.when((z < NZ - 1) & (z >= m // nc))
        def _():
            fwd(m).wait_send()

        @pl.when((z > 0) & (NZ - 1 - z >= m // nc))
        def _():
            bwd(m).wait_send()

    d_m(p).wait_send()

    @pl.when(xx == 0)
    def _():
        d_x().wait_send()

    @pl.when(z == 0)
    def _():
        for to in range(1, NZ):
            r_z(to).wait_send()

            @pl.when(xx == 0)
            def _():
                d_z(to).wait_send()

    for k in range(SWEEPS):
        @pl.when(has_prev)
        def _():
            h_prev(k).wait_send()

        @pl.when(has_next)
        def _():
            h_next(k).wait_send()


def finish_kernel(nc, s0, s1, s2, s3, left, g, trail, hour, out, trail_out, hour_out, sem):
    s = (s0, s1, s2, s3)
    z = lax.axis_index("tm")
    pairs = nc // 2

    def put(q, j):
        for t in (2 * j, 2 * j + 1):
            pltpu.make_async_copy(s[q].at[t], out.at[:, q * nc + t, 0, :], sem.at[q * nc + t]).start()

    def ready(q, j):
        fore = (z - 1 - q) * pairs + j
        back = (q - z - 1) * pairs + j
        return (z == q) | ((z > q) & (fore < EARLY)) | ((z < q) & (back < EARLY))

    for q in range(NZ):
        for j in range(pairs):
            @pl.when(ready(q, j))
            def _():
                put(q, j)

    trail_out[...] = trail[...]
    hour_out[...] = hour[...]
    for q in range(NZ):
        for j in range(pairs):
            @pl.when(jnp.logical_not(ready(q, j)))
            def _():
                def body(b, carry):
                    at = pl.ds(pl.multiple_of(b * 2 * W, 2 * W), 2 * W)
                    u = product(left[at, :], g[q * pairs + j])
                    s[q][2 * j, at, :] -= u[:, :W]
                    s[q][2 * j + 1, at, :] -= u[:, W:]
                    return carry
                lax.fori_loop(0, 2 * nc, body, 0)
                put(q, j)

    for q in range(NZ):
        for t in range(nc):
            pltpu.make_async_copy(s[q].at[t], out.at[:, q * nc + t, 0, :], sem.at[q * nc + t]).wait()


def eliminate(schur, link_rhs, hour_rhs, link_cols, link_coef, hour_inverse, couple_prev, couple_next):
    rows_here, tiles, _, w = schur.shape
    nc = tiles // NZ
    pairs = tiles // 2
    total = (NZ - 1) * nc
    dma = pltpu.SemaphoreType.DMA
    f32, bf16 = jnp.float32, jnp.bfloat16
    vmem = pl.BlockSpec(memory_space=pltpu.VMEM)
    hbm = pl.BlockSpec(memory_space=pl.ANY)
    made = pl.pallas_call(
        functools.partial(panel_kernel, nc),
        out_shape=tuple(pltpu.VMEM((nc, rows_here, w), f32) for _ in range(NZ)) + (
            pltpu.VMEM((rows_here, 4 * w), bf16),
            pltpu.VMEM((pairs, 4 * w, 2 * w), bf16),
            pltpu.VMEM((rows_here // w, w), f32),
            pltpu.VMEM((1, 2 * w), f32),
        ),
        in_specs=[hbm] + [vmem] * 7,
        out_specs=(vmem,) * (NZ + 4),
        scratch_shapes=[
            pltpu.VMEM((2, 2 * nc, 2 * w, w), f32),
            pltpu.VMEM((2, NZ, nc // 2, 2 * w, w), f32),
            pltpu.VMEM((2, 2 * w, w), f32),
            pltpu.VMEM((8, w), f32),
            pltpu.VMEM((SWEEPS + 1, 8, 2 * w), f32),
            pltpu.VMEM((SWEEPS, 2, 8, 2 * w), f32),
            pltpu.VMEM((2 * w, 2 * w), f32),
            dma((2 * nc,)), dma((tiles,)), dma((nc,)),
            dma((2 * nc,)), dma((2 * nc,)), dma((2 * nc,)), dma((2 * nc,)),
            dma((total,)), dma((total,)), dma((total,)), dma((total,)),
            dma((NZ - 1,)), dma, dma, dma, dma, dma, dma((NZ - 1,)), dma,
            dma((SWEEPS, 2)), dma((SWEEPS, 2)),
        ],
        compiler_params=pltpu.CompilerParams(
            collective_id=0, has_side_effects=True, vmem_limit_bytes=11 * 1024 * 1024),
    )(schur, link_rhs.reshape(rows_here // w, w), hour_rhs, link_cols, link_coef, hour_inverse,
      couple_prev, couple_next)
    out, trail, hour = pl.pallas_call(
        functools.partial(finish_kernel, nc),
        out_shape=(
            jax.ShapeDtypeStruct(schur.shape, f32),
            jax.ShapeDtypeStruct((rows_here // w, w), f32),
            jax.ShapeDtypeStruct((1, 2 * w), f32),
        ),
        in_specs=[vmem] * (NZ + 4),
        out_specs=(hbm, vmem, vmem),
        scratch_shapes=[dma((tiles,))],
        compiler_params=pltpu.CompilerParams(vmem_limit_bytes=4 * 1024 * 1024),
    )(*made)
    return out, trail.reshape(-1), hour


def panels_by_step(schur_now, rhs_now):
    rows_here = schur_now.shape[0]
    tiles_here = schur_now.shape[1]
    width = schur_now.shape[3]
    factors = lax.axis_size("factor")
    row_start = lax.axis_index("tm") * rows_here
    global_rows = row_start + jnp.arange(rows_here, dtype=jnp.int32)
    factor_here = lax.axis_index("factor")
    solved = []
    for panel_id in range(PANELS):
        column_tile = panel_id // factors
        owner_index = panel_id % factors
        own_cols = schur_now[:, column_tile, 0, :]
        panel_cols = spread(own_cols, "factor", owner_index)
        panel_first = panel_id * width
        picker = (
            global_rows[:, None] - panel_first == jnp.arange(width, dtype=jnp.int32)[None, :]
        ).astype(jnp.float32)
        block_part = jnp.dot(picker.T, panel_cols, precision=lax.Precision.HIGHEST)
        rhs_part = jnp.dot(picker.T, rhs_now, precision=lax.Precision.HIGHEST)
        diag_block, rhs_segment = lax.psum((block_part, rhs_part), "tm")
        lower_block = jnp.linalg.cholesky(diag_block)
        factor_rows = jax.scipy.linalg.solve_triangular(lower_block, panel_cols.T, lower=True).T
        factor_rows = jnp.where(
            (global_rows < panel_first)[:, None], jnp.zeros_like(factor_rows), factor_rows
        )
        all_factor = lax.all_gather(factor_rows, "tm", axis=0, tiled=True)
        grouped = all_factor.reshape(tiles_here, factors, width, width)
        my_tiles = lax.dynamic_index_in_dim(grouped, factor_here, 1, keepdims=False)
        link_step = jax.scipy.linalg.solve_triangular(lower_block, rhs_segment, lower=True)
        rhs_now = rhs_now - jnp.dot(factor_rows, link_step, precision=lax.Precision.HIGHEST)
        update = jnp.einsum("rk,tck->rtc", factor_rows, my_tiles, precision=lax.Precision.HIGHEST)
        schur_now = schur_now - update[:, :, None, :]
        solved.append(link_step)
    return schur_now, rhs_now, jnp.concatenate(solved)


def shards(
    schur_matrix, link_rhs, hour_rhs, link_cols, link_coef, hour_inverse, couple_prev, couple_next
):
    rows_here, tiles, _, width = schur_matrix.shape
    zs = lax.axis_size("tm")
    fused = lax.axis_size("factor") == 4 and zs == 4 and width == 128 and hour_rhs.shape == (1, 256)
    fused = fused and tiles % (2 * zs) == 0 and rows_here * zs == tiles * 4 * width and rows_here <= 3072
    if fused:
        return eliminate(
            schur_matrix, link_rhs, hour_rhs, link_cols, link_coef, hour_inverse, couple_prev, couple_next)
    schur_now, rhs_now, link_values = panels_by_step(schur_matrix, link_rhs)
    one_hot = (
        link_cols[:, :, None] == jnp.arange(PANELS * width, dtype=jnp.int32)[None, None, :]
    ).astype(jnp.float32)
    looked = jnp.einsum("hik,k->hi", one_hot, link_values, precision=lax.Precision.HIGHEST)
    target = hour_rhs - link_coef * looked
    hour_state = jnp.einsum("hik,hk->hi", hour_inverse, target, precision=lax.Precision.HIGHEST)
    for sweep_id in range(SWEEPS):
        border_pairs = jnp.concatenate((hour_state[:, :BW], hour_state[:, -BW:]), axis=1)
        padded = with_halo(border_pairs, ((("tm", "factor"), 0),), 1)
        prev_last = padded[:-2, BW:]
        next_first = padded[2:, :BW]
        coupling = jnp.einsum("hbi,hb->hi", couple_prev, prev_last, precision=lax.Precision.HIGHEST)
        coupling = coupling + jnp.einsum(
            "hbi,hb->hi", couple_next, next_first, precision=lax.Precision.HIGHEST
        )
        hour_state = jnp.einsum(
            "hik,hk->hi", hour_inverse, target - coupling, precision=lax.Precision.HIGHEST
        )
    return (schur_now, rhs_now, hour_state)


def solution(mesh):
    placed = (
        P(("parts", "tm"), None, "factor", None),
        P(("parts", "tm")),
        P(("parts", "tm", "factor"), None),
        P(("parts", "tm", "factor"), None),
        P(("parts", "tm", "factor"), None),
        P(("parts", "tm", "factor"), None, None),
        P(("parts", "tm", "factor"), None, None),
        P(("parts", "tm", "factor"), None, None),
    )
    return jax.shard_map(
        shards,
        mesh=mesh,
        in_specs=placed,
        out_specs=(
            P(("parts", "tm"), None, "factor", None),
            P(("parts", "tm")),
            P(("parts", "tm", "factor"), None),
        ),
        check_vma=False,
    )
```

```python
import functools

import jax
import jax.numpy as jnp
from jax import lax
from jax.experimental import pallas as pl
from jax.experimental.pallas import tpu as pltpu
from jax.sharding import PartitionSpec as P

PANELS = 2
BW = 2
SWEEPS = 2
HIGH = lax.Precision.HIGHEST
MESH = pl.DeviceIdType.MESH


def spread(array, axis, root):
    mine = lax.axis_index(axis) == root
    return lax.psum(jnp.where(mine, array, jnp.zeros_like(array)), axis)


def with_halo(cells, sides, width):
    for axis, dim in sides:
        count = lax.axis_size(axis)
        ends = count - 1
        head = lax.slice_in_dim(cells, 0, width, axis=dim)
        tail = lax.slice_in_dim(cells, cells.shape[dim] - width, cells.shape[dim], axis=dim)
        cells = jnp.concatenate(
            [
                lax.ppermute(tail, axis, [(i, (i + 1) % count) for i in range(ends)]),
                cells,
                lax.ppermute(head, axis, [((i + 1) % count, i) for i in range(ends)]),
            ],
            axis=dim,
        )
    return cells


W = 128
NZ = 4
Z_OPEN = 3
X_OPEN = 2
EARLY = 3


def across(a, b):
    return lax.dot_general(
        a, b, (((1,), (1,)), ((), ())), precision=HIGH, preferred_element_type=jnp.float32)


def matmul(a, b):
    return jnp.dot(a, b, precision=HIGH, preferred_element_type=jnp.float32)


def split(a):
    high = a.astype(jnp.bfloat16)
    return high, (a - high.astype(jnp.float32)).astype(jnp.bfloat16)


def chol_inverse(block, hooks):
    count = W // 8
    rows = [block[8 * i:8 * i + 8, :] for i in range(count)]
    lane = lax.broadcasted_iota(jnp.int32, (8, W), 1)
    sub = lax.broadcasted_iota(jnp.int32, (8, W), 0)
    for b in range(count):
        j0 = 8 * b
        here = (lane >= j0) & (lane < j0 + 8)
        p = rows[b]
        piv = [jnp.broadcast_to(p[:, j0 + t:j0 + t + 1], (8, W)) for t in range(8)]
        p = jnp.where(here, jnp.where(lane - j0 == sub, 1.0, 0.0), p)
        done = p
        for t in range(8):
            d = piv[t][t:t + 1, :]
            r = p[t:t + 1, :]
            done = jnp.where(sub == t, r * lax.rsqrt(d), done)
            inv = 1.0 / d
            rr = r * inv
            p = jnp.where(sub == t, rr, p - piv[t] * rr)
            for u in range(t + 1, 8):
                bu = piv[u][t:t + 1, :] * inv
                piv[u] = jnp.where(sub == t, bu, piv[u] - piv[t] * bu)
        for i in range(b + 1, count):
            old = rows[i]
            now = jnp.where(here, 0.0, old)
            for t in range(8):
                now = now - old[:, j0 + t:j0 + t + 1] * p[t:t + 1, :]
            rows[i] = now
        rows[b] = done
        if b in hooks:
            hooks[b]()
    full = jnp.concatenate(rows, axis=0)
    low = lax.broadcasted_iota(jnp.int32, (W, W), 0) >= lax.broadcasted_iota(jnp.int32, (W, W), 1)
    return jnp.where(low, full, 0.0)


def product(left, right):
    high = left[:, :2 * W]
    rows = jnp.concatenate([high, high, left[:, 2 * W:]], axis=1)
    first = right[:2 * W, :]
    cols = jnp.concatenate([first, right[2 * W:, :], first], axis=0)
    return jnp.dot(rows, cols, preferred_element_type=jnp.float32)


def pair_update(s, left, g, q, j, pairs, blocks, among):
    right = g.at[q * pairs + j]
    for qq in among:
        @pl.when(q == qq)
        def _():
            def body(b, carry):
                at = pl.ds(pl.multiple_of(b * 2 * W, 2 * W), 2 * W)
                u = product(left[at, :], right[...])
                s[qq][2 * j, at, :] -= u[:, :W]
                s[qq][2 * j + 1, at, :] -= u[:, W:]
                return carry
            lax.fori_loop(0, blocks, body, 0, unroll=4)


def panel_kernel(nc, s_hbm, *refs):
    smalls, refs = refs[:7], refs[7:]
    panel_body(nc, s_hbm, smalls, *refs)


def panel_body(
    nc, s_hbm, smalls,
    s0, s1, s2, s3, left, g, trail, hour,
    rhs, h_rhs, h_cols, h_coef, h_inv, c_prev, c_next, cr, cc, dp, rs, hx, hl, inv_ref,
    psem, lsem, ssem, osem, xs, xr, ms, mr, fs, fr, bs, br, dzs, dzr, dxs, dxr, dms, dmr, rss, rsr, hs, hr,
):
    s = (s0, s1, s2, s3)
    f = lax.axis_index("factor")
    z = lax.axis_index("tm")
    p = lax.rem(f, 2)
    q = 1 - p
    xx = lax.div(f, 2)
    mate = {"factor": f + 1 - 2 * p}
    over = {"factor": f + 2 - 4 * xx}
    blocks = 2 * nc
    pairs = nc // 2

    def remote(src, dst, send, recv, device):
        return pltpu.make_async_remote_copy(
            src_ref=src, dst_ref=dst, send_sem=send, recv_sem=recv, device_id=device, device_id_type=MESH)

    def load(b):
        return pltpu.make_async_copy(
            s_hbm.at[b * 2 * W:(b + 1) * 2 * W, 0, 0, :], cr.at[p, b], lsem.at[b])

    def tile_in(t):
        return pltpu.make_async_copy(s_hbm.at[:, t, 0, :], s[t // nc].at[t % nc], ssem.at[t])

    def xcopy(b):
        return remote(cr.at[p, b], cr.at[p, b], xs.at[b], xr.at[b], over)

    def mcopy(panel, b):
        return remote(cr.at[panel, b], cr.at[panel, b], ms.at[b], mr.at[b], mate)

    def slot(quarter, c):
        return cc.at[:, quarter, c // 2, (c % 2) * W:(c % 2 + 1) * W]

    def mine(c):
        return cr.at[:, 2 * c + xx, pl.ds(pl.multiple_of(p * W, W), W)]

    def own_copy(c):
        return pltpu.make_async_copy(mine(c), slot(z, c), osem.at[c])

    def fwd(m):
        c = m % nc
        where = slot(z - m // nc, c)
        return remote(mine(c) if m < nc else where, where, fs.at[m], fr.at[m], {"tm": z + 1})

    def bwd(m):
        c = m % nc
        where = slot(z + m // nc, c)
        return remote(mine(c) if m < nc else where, where, bs.at[m], br.at[m], {"tm": z - 1})

    def fwd_in(m):
        where = slot(z - 1 - m // nc, m % nc)
        return remote(where, where, fs.at[m], fr.at[m], {"tm": z - 1})

    def bwd_in(m):
        where = slot(z + 1 + m // nc, m % nc)
        return remote(where, where, bs.at[m], br.at[m], {"tm": z + 1})

    total = (NZ - 1) * nc

    def z_send(m):
        if not 0 <= m < total:
            return
        step = m // nc
        if step == 0:
            own_copy(m).start()

        @pl.when((z < NZ - 1) & (z >= step))
        def _():
            if step > 0:
                fwd_in(m - nc).wait_recv()
            if m >= Z_OPEN:
                fwd(m - Z_OPEN).wait_send()
            fwd(m).start()

        @pl.when((z > 0) & (NZ - 1 - z >= step))
        def _():
            if step > 0:
                bwd_in(m - nc).wait_recv()
            if m >= Z_OPEN:
                bwd(m - Z_OPEN).wait_send()
            bwd(m).start()

    def take(m):
        @pl.when(z == NZ - 1)
        def _():
            fwd_in(m).wait_recv()

        @pl.when(z == 0)
        def _():
            bwd_in(m).wait_recv()

    def x_block(n):
        return 2 * n + 1 if n < nc else 2 * (n - nc)

    def x_send(n):
        if n < 2 * nc:
            @pl.when(xx == 0)
            def _():
                if n >= X_OPEN:
                    xcopy(x_block(n - X_OPEN)).wait_send()
                xcopy(x_block(n)).start()

    def x1(c):
        @pl.when(xx == 1)
        def _():
            xcopy(2 * c + 1).wait_recv()
            mcopy(p, 2 * c + 1).start()
            mcopy(q, 2 * c + 1).wait_recv()

    def x0(c):
        @pl.when(xx == 1)
        def _():
            xcopy(2 * c).wait_recv()
            mcopy(p, 2 * c).start()
            mcopy(q, 2 * c).wait_recv()

    def d_z(to):
        return remote(cr.at[p, 0], dp.at[p], dzs.at[to - 1], dzr, {"tm": to})

    def r_z(to):
        return remote(rhs.at[0:8], rs, rss.at[to - 1], rsr, {"tm": to})

    def d_x():
        return remote(dp.at[p], dp.at[p], dxs, dxr, over)

    def d_m(panel):
        return remote(dp.at[panel], dp.at[panel], dms, dmr, mate)

    has_prev = (z > 0) | (f > 0)
    has_next = (z < NZ - 1) | (f < 3)

    def h_prev(k):
        return remote(hx.at[k], hl.at[k, 1], hs.at[k, 0], hr.at[k, 1],
                      {"tm": jnp.where(f > 0, z, z - 1), "factor": jnp.where(f > 0, f - 1, 3)})

    def h_next(k):
        return remote(hx.at[k], hl.at[k, 0], hs.at[k, 1], hr.at[k, 0],
                      {"tm": jnp.where(f < 3, z, z + 1), "factor": jnp.where(f < 3, f + 1, 0)})

    @pl.when(xx == 0)
    def _():
        for b in range(blocks):
            load(b).start()

    hl[...] = jnp.zeros_like(hl)
    held = (rhs, h_rhs, h_cols, h_coef, h_inv, c_prev, c_next)
    fetch = [pltpu.make_async_copy(a, b, psem.at[i]) for i, (a, b) in enumerate(zip(smalls, held))]
    for one in fetch:
        one.start()

    barrier = pltpu.get_barrier_semaphore()

    def greet(device):
        pl.semaphore_signal(barrier, inc=1, device_id=device, device_id_type=MESH)

    greet(mate)
    greet(over)
    for step in range(1, NZ):
        greet({"tm": lax.rem(z + step, NZ)})
    middle = (f == 1) | (f == 2)
    up = (f == 3) & (z < NZ - 1)
    down = (f == 0) & (z > 0)

    @pl.when(middle)
    def _():
        greet({"factor": 3 - f})

    @pl.when(up)
    def _():
        greet({"tm": z + 1, "factor": 0})

    @pl.when(down)
    def _():
        greet({"tm": z - 1, "factor": 3})

    pl.semaphore_wait(barrier, NZ + 1 + jnp.where(middle | up | down, 1, 0))

    fetch[0].wait()

    @pl.when(z == 0)
    def _():
        for to in range(1, NZ):
            r_z(to).start()
        rs[...] = rhs[0:8, :]

    def x_send_now(n):
        xcopy(x_block(n)).start()

    @pl.when(xx == 0)
    def _():
        load(0).wait()

        @pl.when(z == 0)
        def _():
            for to in range(NZ - 1, 0, -1):
                d_z(to).start()
            dp[p] = cr[p, 0]
            d_x().start()
            d_m(p).start()

        for c in range(nc):
            if c > 0:
                load(2 * c).wait()
            load(2 * c + 1).wait()
            if c < X_OPEN:
                x_send_now(c)
            mcopy(p, 2 * c).start()
            mcopy(p, 2 * c + 1).start()
        for c in range(nc):
            mcopy(q, 2 * c).wait_recv()
            mcopy(q, 2 * c + 1).wait_recv()

    @pl.when((xx == 0) & (z == 0))
    def _():
        for to in range(NZ - 1, 0, -1):
            d_z(to).wait_send()

    def service(n):
        if n < nc:
            x1(n)
        z_send(n)
        if n >= X_OPEN:
            x_send(n)

    service(0)
    service(1)
    for t in range(NZ * nc):
        tile_in(t).start()
    service(2)

    @pl.when((xx == 0) & (z > 0))
    def _():
        d_z(1).wait_recv()
        d_x().start()
        d_m(p).start()

    @pl.when(xx == 1)
    def _():
        d_x().wait_recv()
        d_m(p).start()

    d_m(q).wait_recv()

    top = chol_inverse(dp[0, 0:W, :], {4: lambda: service(3), 11: lambda: service(4)})

    service(5)
    side = across(dp[0, W:, :], top)
    low = chol_inverse(
        dp[1, W:, :] - across(side, side), {3: lambda: service(6), 10: lambda: service(7)})
    mixed = -matmul(low, matmul(side, top))
    service(8)
    inv_ref[:W, :W] = top
    inv_ref[:W, W:] = jnp.zeros((W, W), jnp.float32)
    inv_ref[W:, :W] = mixed
    inv_ref[W:, W:] = low

    @pl.when(z > 0)
    def _():
        r_z(1).wait_recv()

    for one in fetch[1:]:
        one.wait()
    seg = jnp.concatenate([rs[0:1, :], rs[1:2, :]], axis=1)
    link = across(jnp.broadcast_to(seg, (8, 2 * W)), inv_ref[...])
    hot = (lax.broadcasted_iota(jnp.int32, (2 * W, 2 * W), 0) == h_cols[...]).astype(jnp.float32)
    target = h_rhs[...] - h_coef[...] * matmul(link, hot)

    def solve(k, want):
        hx[k] = across(want, h_inv[0])
        if k < SWEEPS:
            @pl.when(has_prev)
            def _():
                h_prev(k).start()

            @pl.when(has_next)
            def _():
                h_next(k).start()

    def sweep(k):
        @pl.when(has_prev)
        def _():
            h_next(k).wait_recv()

        @pl.when(has_next)
        def _():
            h_prev(k).wait_recv()

        before = hl[k, 0]
        after = hl[k, 1]
        coupling = before[:, 2 * W - 2:2 * W - 1] * c_prev[0, 0:1, :]
        coupling = coupling + before[:, 2 * W - 1:2 * W] * c_prev[0, 1:2, :]
        coupling = coupling + after[:, 0:1] * c_next[0, 0:1, :]
        coupling = coupling + after[:, 1:2] * c_next[0, 1:2, :]
        solve(k + 1, target - coupling)

    solve(0, target)

    def frow(b):
        fr_ = across(cr[0, b], inv_ref[:, :W]) + across(cr[1, b], inv_ref[:, W:])
        if not isinstance(b, int) or b == 0:
            row = lax.broadcasted_iota(jnp.int32, fr_.shape, 0) + (z * blocks + b) * 2 * W
            depth = lax.broadcasted_iota(jnp.int32, fr_.shape, 1)
            fr_ = jnp.where((row < W) & (depth >= W), 0.0, fr_)
        high, rest = split(fr_)
        at = pl.ds(b * 2 * W, 2 * W)
        left[at, :2 * W] = high
        left[at, 2 * W:] = rest
        gone = across(link, fr_)
        trail[pl.ds(2 * b, 1), :] = rhs[pl.ds(2 * b, 1), :] - gone[0:1, :W]
        trail[pl.ds(2 * b + 1, 1), :] = rhs[pl.ds(2 * b + 1, 1), :] - gone[0:1, W:]

    def fcol(quarter, j):
        gg = across(inv_ref[:, :W], cc[0, quarter, j]) + across(inv_ref[:, W:], cc[1, quarter, j])
        limit = jnp.where((quarter == 0) & (j == 0) & (f == 0), W, 0)
        depth = lax.broadcasted_iota(jnp.int32, gg.shape, 0)
        col = lax.broadcasted_iota(jnp.int32, gg.shape, 1)
        high, rest = split(jnp.where((depth >= W) & (col < limit), 0.0, gg))
        at = quarter * pairs + j
        g[at, :2 * W, :] = high
        g[at, 2 * W:, :] = rest

    def received(n, update):
        step, j = n // pairs, n % pairs

        @pl.when(z > step)
        def _():
            fcol(z - 1 - step, j)
            if update:
                pair_update(s, left, g, z - 1 - step, j, pairs, blocks, range(NZ - 1 - step))

        @pl.when(z < NZ - 1 - step)
        def _():
            fcol(z + 1 + step, j)
            if update:
                pair_update(s, left, g, z + 1 + step, j, pairs, blocks, range(1 + step, NZ))

    upcoming = 9
    for c in range(nc):
        frow(2 * c + 1)
        if c % 3 == 2:
            service(upcoming)
            upcoming += 1
    sweep(0)
    for c in range(nc):
        x0(c)
        frow(2 * c)
        if c % 3 == 2:
            service(upcoming)
            upcoming += 1
    for c in range(nc):
        own_copy(c).wait()
    for t in range(NZ * nc):
        tile_in(t).wait()
    for j in range(pairs):
        fcol(z, j)
        pair_update(s, left, g, z, j, pairs, blocks, range(NZ))
        service(upcoming)
        upcoming += 1
        if j == 0:
            sweep(1)
    hour[...] = hx[SWEEPS, 0:1, :]
    for n in range(total // 2):
        while upcoming < total and upcoming < 2 * n + 2 + nc:
            service(upcoming)
            upcoming += 1
        take(2 * n)
        take(2 * n + 1)
        received(n, n < EARLY)
        if upcoming < total:
            service(upcoming)
            upcoming += 1

    for b in range(blocks):
        mcopy(p, b).wait_send()

    @pl.when(xx == 0)
    def _():
        for n in range(2 * nc - X_OPEN, 2 * nc):
            xcopy(x_block(n)).wait_send()

    for m in range(total):
        step, later = m // nc, (m + Z_OPEN) // nc
        if later > step:
            @pl.when((z < NZ - 1) & (z >= step) & (z < later))
            def _():
                fwd(m).wait_send()

            @pl.when((z > 0) & (NZ - 1 - z >= step) & (NZ - 1 - z < later))
            def _():
                bwd(m).wait_send()

    d_m(p).wait_send()

    @pl.when(xx == 0)
    def _():
        d_x().wait_send()

    @pl.when(z == 0)
    def _():
        for to in range(1, NZ):
            r_z(to).wait_send()

    for k in range(SWEEPS):
        @pl.when(has_prev)
        def _():
            h_prev(k).wait_send()

        @pl.when(has_next)
        def _():
            h_next(k).wait_send()


def finish_kernel(nc, s0, s1, s2, s3, left, g, trail, hour, out, trail_out, hour_out, sem):
    s = (s0, s1, s2, s3)
    z = lax.axis_index("tm")
    pairs = nc // 2

    def put(q, j):
        for t in (2 * j, 2 * j + 1):
            pltpu.make_async_copy(s[q].at[t], out.at[:, q * nc + t, 0, :], sem.at[q * nc + t]).start()

    def ready(q, j):
        fore = (z - 1 - q) * pairs + j
        back = (q - z - 1) * pairs + j
        return (z == q) | ((z > q) & (fore < EARLY)) | ((z < q) & (back < EARLY))

    for q in range(NZ):
        for j in range(pairs):
            @pl.when(ready(q, j))
            def _():
                put(q, j)

    trail_out[...] = trail[...]
    hour_out[...] = hour[...]
    for q in range(NZ):
        for j in range(pairs):
            @pl.when(jnp.logical_not(ready(q, j)))
            def _():
                def body(b, carry):
                    at = pl.ds(pl.multiple_of(b * 2 * W, 2 * W), 2 * W)
                    u = product(left[at, :], g[q * pairs + j])
                    s[q][2 * j, at, :] -= u[:, :W]
                    s[q][2 * j + 1, at, :] -= u[:, W:]
                    return carry
                lax.fori_loop(0, 2 * nc, body, 0, unroll=2 * nc)
                put(q, j)

    for q in range(NZ):
        for t in range(nc):
            pltpu.make_async_copy(s[q].at[t], out.at[:, q * nc + t, 0, :], sem.at[q * nc + t]).wait()


def eliminate(schur, link_rhs, hour_rhs, link_cols, link_coef, hour_inverse, couple_prev, couple_next):
    rows_here, tiles, _, w = schur.shape
    nc = tiles // NZ
    pairs = tiles // 2
    total = (NZ - 1) * nc
    dma = pltpu.SemaphoreType.DMA
    f32, bf16 = jnp.float32, jnp.bfloat16
    vmem = pl.BlockSpec(memory_space=pltpu.VMEM)
    hbm = pl.BlockSpec(memory_space=pl.ANY)
    smalls = (link_rhs.reshape(rows_here // w, w), hour_rhs, link_cols, link_coef, hour_inverse,
              couple_prev, couple_next)
    made = pl.pallas_call(
        functools.partial(panel_kernel, nc),
        out_shape=tuple(pltpu.VMEM((nc, rows_here, w), f32) for _ in range(NZ)) + (
            pltpu.VMEM((rows_here, 4 * w), bf16),
            pltpu.VMEM((pairs, 4 * w, 2 * w), bf16),
            pltpu.VMEM((rows_here // w, w), f32),
            pltpu.VMEM((1, 2 * w), f32),
        ),
        in_specs=[pl.BlockSpec(memory_space=pltpu.HBM)] * 8,
        out_specs=(vmem,) * (NZ + 4),
        scratch_shapes=[pltpu.VMEM(a.shape, a.dtype) for a in smalls] + [
            pltpu.VMEM((2, 2 * nc, 2 * w, w), f32),
            pltpu.VMEM((2, NZ, nc // 2, 2 * w, w), f32),
            pltpu.VMEM((2, 2 * w, w), f32),
            pltpu.VMEM((8, w), f32),
            pltpu.VMEM((SWEEPS + 1, 8, 2 * w), f32),
            pltpu.VMEM((SWEEPS, 2, 8, 2 * w), f32),
            pltpu.VMEM((2 * w, 2 * w), f32),
            dma((7,)), dma((2 * nc,)), dma((tiles,)), dma((nc,)),
            dma((2 * nc,)), dma((2 * nc,)), dma((2 * nc,)), dma((2 * nc,)),
            dma((total,)), dma((total,)), dma((total,)), dma((total,)),
            dma((NZ - 1,)), dma, dma, dma, dma, dma, dma((NZ - 1,)), dma,
            dma((SWEEPS, 2)), dma((SWEEPS, 2)),
        ],
        compiler_params=pltpu.CompilerParams(
            collective_id=0, has_side_effects=True, vmem_limit_bytes=12 * 1024 * 1024),
    )(schur, *smalls)
    out, trail, hour = pl.pallas_call(
        functools.partial(finish_kernel, nc),
        out_shape=(
            jax.ShapeDtypeStruct(schur.shape, f32),
            jax.ShapeDtypeStruct((rows_here // w, w), f32),
            jax.ShapeDtypeStruct((1, 2 * w), f32),
        ),
        in_specs=[vmem] * (NZ + 4),
        out_specs=(hbm, vmem, vmem),
        scratch_shapes=[dma((tiles,))],
        compiler_params=pltpu.CompilerParams(vmem_limit_bytes=4 * 1024 * 1024),
    )(*made)
    return out, trail.reshape(-1), hour


def panels_by_step(schur_now, rhs_now):
    rows_here = schur_now.shape[0]
    tiles_here = schur_now.shape[1]
    width = schur_now.shape[3]
    factors = lax.axis_size("factor")
    row_start = lax.axis_index("tm") * rows_here
    global_rows = row_start + jnp.arange(rows_here, dtype=jnp.int32)
    factor_here = lax.axis_index("factor")
    solved = []
    for panel_id in range(PANELS):
        column_tile = panel_id // factors
        owner_index = panel_id % factors
        own_cols = schur_now[:, column_tile, 0, :]
        panel_cols = spread(own_cols, "factor", owner_index)
        panel_first = panel_id * width
        picker = (
            global_rows[:, None] - panel_first == jnp.arange(width, dtype=jnp.int32)[None, :]
        ).astype(jnp.float32)
        block_part = jnp.dot(picker.T, panel_cols, precision=lax.Precision.HIGHEST)
        rhs_part = jnp.dot(picker.T, rhs_now, precision=lax.Precision.HIGHEST)
        diag_block, rhs_segment = lax.psum((block_part, rhs_part), "tm")
        lower_block = jnp.linalg.cholesky(diag_block)
        factor_rows = jax.scipy.linalg.solve_triangular(lower_block, panel_cols.T, lower=True).T
        factor_rows = jnp.where(
            (global_rows < panel_first)[:, None], jnp.zeros_like(factor_rows), factor_rows
        )
        all_factor = lax.all_gather(factor_rows, "tm", axis=0, tiled=True)
        grouped = all_factor.reshape(tiles_here, factors, width, width)
        my_tiles = lax.dynamic_index_in_dim(grouped, factor_here, 1, keepdims=False)
        link_step = jax.scipy.linalg.solve_triangular(lower_block, rhs_segment, lower=True)
        rhs_now = rhs_now - jnp.dot(factor_rows, link_step, precision=lax.Precision.HIGHEST)
        update = jnp.einsum("rk,tck->rtc", factor_rows, my_tiles, precision=lax.Precision.HIGHEST)
        schur_now = schur_now - update[:, :, None, :]
        solved.append(link_step)
    return schur_now, rhs_now, jnp.concatenate(solved)


def shards(
    schur_matrix, link_rhs, hour_rhs, link_cols, link_coef, hour_inverse, couple_prev, couple_next
):
    rows_here, tiles, _, width = schur_matrix.shape
    zs = lax.axis_size("tm")
    fused = lax.axis_size("factor") == 4 and zs == 4 and width == 128 and hour_rhs.shape == (1, 256)
    fused = fused and tiles % (2 * zs) == 0 and rows_here * zs == tiles * 4 * width and rows_here <= 3072
    if fused:
        return eliminate(
            schur_matrix, link_rhs, hour_rhs, link_cols, link_coef, hour_inverse, couple_prev, couple_next)
    schur_now, rhs_now, link_values = panels_by_step(schur_matrix, link_rhs)
    one_hot = (
        link_cols[:, :, None] == jnp.arange(PANELS * width, dtype=jnp.int32)[None, None, :]
    ).astype(jnp.float32)
    looked = jnp.einsum("hik,k->hi", one_hot, link_values, precision=lax.Precision.HIGHEST)
    target = hour_rhs - link_coef * looked
    hour_state = jnp.einsum("hik,hk->hi", hour_inverse, target, precision=lax.Precision.HIGHEST)
    for sweep_id in range(SWEEPS):
        border_pairs = jnp.concatenate((hour_state[:, :BW], hour_state[:, -BW:]), axis=1)
        padded = with_halo(border_pairs, ((("tm", "factor"), 0),), 1)
        prev_last = padded[:-2, BW:]
        next_first = padded[2:, :BW]
        coupling = jnp.einsum("hbi,hb->hi", couple_prev, prev_last, precision=lax.Precision.HIGHEST)
        coupling = coupling + jnp.einsum(
            "hbi,hb->hi", couple_next, next_first, precision=lax.Precision.HIGHEST
        )
        hour_state = jnp.einsum(
            "hik,hk->hi", hour_inverse, target - coupling, precision=lax.Precision.HIGHEST
        )
    return (schur_now, rhs_now, hour_state)


def solution(mesh):
    placed = (
        P(("parts", "tm"), None, "factor", None),
        P(("parts", "tm")),
        P(("parts", "tm", "factor"), None),
        P(("parts", "tm", "factor"), None),
        P(("parts", "tm", "factor"), None),
        P(("parts", "tm", "factor"), None, None),
        P(("parts", "tm", "factor"), None, None),
        P(("parts", "tm", "factor"), None, None),
    )
    return jax.shard_map(
        shards,
        mesh=mesh,
        in_specs=placed,
        out_specs=(
            P(("parts", "tm"), None, "factor", None),
            P(("parts", "tm")),
            P(("parts", "tm", "factor"), None),
        ),
        check_vma=False,
    )
```

```python
import functools

import jax
import jax.numpy as jnp
from jax import lax
from jax.experimental import pallas as pl
from jax.experimental.pallas import tpu as pltpu
from jax.sharding import PartitionSpec as P

PANELS = 2
BW = 2
SWEEPS = 2
HIGH = lax.Precision.HIGHEST
MESH = pl.DeviceIdType.MESH


def spread(array, axis, root):
    mine = lax.axis_index(axis) == root
    return lax.psum(jnp.where(mine, array, jnp.zeros_like(array)), axis)


def with_halo(cells, sides, width):
    for axis, dim in sides:
        count = lax.axis_size(axis)
        ends = count - 1
        head = lax.slice_in_dim(cells, 0, width, axis=dim)
        tail = lax.slice_in_dim(cells, cells.shape[dim] - width, cells.shape[dim], axis=dim)
        cells = jnp.concatenate(
            [
                lax.ppermute(tail, axis, [(i, (i + 1) % count) for i in range(ends)]),
                cells,
                lax.ppermute(head, axis, [((i + 1) % count, i) for i in range(ends)]),
            ],
            axis=dim,
        )
    return cells


W = 128
NZ = 4
Z_OPEN = 5
X_OPEN = 2
EARLY = 2


def across(a, b):
    return lax.dot_general(
        a, b, (((1,), (1,)), ((), ())), precision=HIGH, preferred_element_type=jnp.float32)


def matmul(a, b):
    return jnp.dot(a, b, precision=HIGH, preferred_element_type=jnp.float32)


def split(a):
    high = a.astype(jnp.bfloat16)
    return high, (a - high.astype(jnp.float32)).astype(jnp.bfloat16)


def chol_inverse(block, hooks):
    count = W // 8
    rows = [block[8 * i:8 * i + 8, :] for i in range(count)]
    lane = lax.broadcasted_iota(jnp.int32, (8, W), 1)
    sub = lax.broadcasted_iota(jnp.int32, (8, W), 0)
    for b in range(count):
        j0 = 8 * b
        here = (lane >= j0) & (lane < j0 + 8)
        p = rows[b]
        piv = [jnp.broadcast_to(p[:, j0 + t:j0 + t + 1], (8, W)) for t in range(8)]
        p = jnp.where(here, jnp.where(lane - j0 == sub, 1.0, 0.0), p)
        done = p
        for t in range(8):
            d = piv[t][t:t + 1, :]
            r = p[t:t + 1, :]
            done = jnp.where(sub == t, r * lax.rsqrt(d), done)
            inv = 1.0 / d
            rr = r * inv
            p = jnp.where(sub == t, rr, p - piv[t] * rr)
            for u in range(t + 1, 8):
                bu = piv[u][t:t + 1, :] * inv
                piv[u] = jnp.where(sub == t, bu, piv[u] - piv[t] * bu)
        for i in range(b + 1, count):
            old = rows[i]
            now = jnp.where(here, 0.0, old)
            for t in range(8):
                now = now - old[:, j0 + t:j0 + t + 1] * p[t:t + 1, :]
            rows[i] = now
        rows[b] = done
        if b in hooks:
            hooks[b]()
    full = jnp.concatenate(rows, axis=0)
    low = lax.broadcasted_iota(jnp.int32, (W, W), 0) >= lax.broadcasted_iota(jnp.int32, (W, W), 1)
    return jnp.where(low, full, 0.0)


def product(left, right):
    high = left[:, :2 * W]
    rows = jnp.concatenate([high, high, left[:, 2 * W:]], axis=1)
    first = right[:2 * W, :]
    cols = jnp.concatenate([first, right[2 * W:, :], first], axis=0)
    return jnp.dot(rows, cols, preferred_element_type=jnp.float32)


def half_update(s, left, g, q, first, last, half, pairs, blocks, among):
    for qq in among:
        @pl.when(q == qq)
        def _():
            @pl.loop(first, last)
            def _(j):
                right = g.at[qq * pairs + j]

                def body(b, carry):
                    at = pl.ds(pl.multiple_of((2 * b + half) * 2 * W, 2 * W), 2 * W)
                    u = product(left[at, :], right[...])
                    s[qq][2 * j, at, :] -= u[:, :W]
                    s[qq][2 * j + 1, at, :] -= u[:, W:]
                    return carry
                lax.fori_loop(0, blocks // 2, body, 0, unroll=blocks // 2)


def panel_kernel(nc, s_hbm, *refs):
    smalls, refs = refs[:7], refs[7:]
    panel_body(nc, s_hbm, smalls, *refs)


def panel_body(
    nc, s_hbm, smalls,
    s0, s1, s2, s3, left, g, trail, hour,
    rhs, h_rhs, h_cols, h_coef, h_inv, c_prev, c_next, cr, cc, dp, rs, hx, hl, inv_ref,
    psem, lsem, ssem, osem, xs, xr, ms, mr, fs, fr, bs, br, dzs, dzr, dxs, dxr, dms, dmr, rss, rsr, hs, hr,
):
    s = (s0, s1, s2, s3)
    f = lax.axis_index("factor")
    z = lax.axis_index("tm")
    p = lax.rem(f, 2)
    q = 1 - p
    xx = lax.div(f, 2)
    mate = {"factor": f + 1 - 2 * p}
    over = {"factor": f + 2 - 4 * xx}
    blocks = 2 * nc
    pairs = nc // 2

    def remote(src, dst, send, recv, device):
        return pltpu.make_async_remote_copy(
            src_ref=src, dst_ref=dst, send_sem=send, recv_sem=recv, device_id=device, device_id_type=MESH)

    def load(b):
        return pltpu.make_async_copy(
            s_hbm.at[b * 2 * W:(b + 1) * 2 * W, 0, 0, :], cr.at[p, b], lsem.at[b])

    def tile_in(t):
        return pltpu.make_async_copy(s_hbm.at[:, t, 0, :], s[t // nc].at[t % nc], ssem.at[t])

    def xcopy(b):
        return remote(cr.at[p, b], cr.at[p, b], xs.at[b], xr.at[b], over)

    def mcopy(panel, b):
        return remote(cr.at[panel, b], cr.at[panel, b], ms.at[b], mr.at[b], mate)

    def slot(quarter, c):
        return cc.at[:, quarter, c // 2, (c % 2) * W:(c % 2 + 1) * W]

    def mine(c):
        return cr.at[:, 2 * c + xx, pl.ds(pl.multiple_of(p * W, W), W)]

    def own_copy(c):
        return pltpu.make_async_copy(mine(c), slot(z, c), osem.at[c])

    def fwd(m):
        c = m % nc
        where = slot(z - m // nc, c)
        return remote(mine(c) if m < nc else where, where, fs.at[m], fr.at[m], {"tm": z + 1})

    def bwd(m):
        c = m % nc
        where = slot(z + m // nc, c)
        return remote(mine(c) if m < nc else where, where, bs.at[m], br.at[m], {"tm": z - 1})

    def fwd_in(m):
        where = slot(z - 1 - m // nc, m % nc)
        return remote(where, where, fs.at[m], fr.at[m], {"tm": z - 1})

    def bwd_in(m):
        where = slot(z + 1 + m // nc, m % nc)
        return remote(where, where, bs.at[m], br.at[m], {"tm": z + 1})

    total = (NZ - 1) * nc

    def z_send(m):
        if not 0 <= m < total:
            return
        step = m // nc
        if step == 0:
            own_copy(m).start()

        @pl.when((z < NZ - 1) & (z >= step))
        def _():
            if step > 0:
                fwd_in(m - nc).wait_recv()
            if m >= Z_OPEN:
                fwd(m - Z_OPEN).wait_send()
            fwd(m).start()

        @pl.when((z > 0) & (NZ - 1 - z >= step))
        def _():
            if step > 0:
                bwd_in(m - nc).wait_recv()
            if m >= Z_OPEN:
                bwd(m - Z_OPEN).wait_send()
            bwd(m).start()

    def take(m):
        @pl.when(z == NZ - 1)
        def _():
            fwd_in(m).wait_recv()

        @pl.when(z == 0)
        def _():
            bwd_in(m).wait_recv()

    def x_block(n):
        return 2 * n + 1 if n < nc else 2 * (n - nc)

    def x_send(n):
        if n < 2 * nc:
            @pl.when(xx == 0)
            def _():
                if X_OPEN <= n < nc:
                    xcopy(x_block(n - X_OPEN)).wait_send()
                xcopy(x_block(n)).start()

    def x1(c):
        @pl.when(xx == 1)
        def _():
            xcopy(2 * c + 1).wait_recv()
            mcopy(p, 2 * c + 1).start()
            mcopy(q, 2 * c + 1).wait_recv()

    def x0(c):
        @pl.when(xx == 1)
        def _():
            xcopy(2 * c).wait_recv()
            mcopy(p, 2 * c).start()
            mcopy(q, 2 * c).wait_recv()

    def d_z(to):
        return remote(cr.at[p, 0], dp.at[p], dzs.at[to - 1], dzr, {"tm": to})

    def r_z(to):
        return remote(rhs.at[0:8], rs, rss.at[to - 1], rsr, {"tm": to})

    def d_x():
        return remote(dp.at[p], dp.at[p], dxs, dxr, over)

    def d_m(panel):
        return remote(dp.at[panel], dp.at[panel], dms, dmr, mate)

    has_prev = (z > 0) | (f > 0)
    has_next = (z < NZ - 1) | (f < 3)

    def h_prev(k):
        return remote(hx.at[k], hl.at[k, 1], hs.at[k, 0], hr.at[k, 1],
                      {"tm": jnp.where(f > 0, z, z - 1), "factor": jnp.where(f > 0, f - 1, 3)})

    def h_next(k):
        return remote(hx.at[k], hl.at[k, 0], hs.at[k, 1], hr.at[k, 0],
                      {"tm": jnp.where(f < 3, z, z + 1), "factor": jnp.where(f < 3, f + 1, 0)})

    @pl.when(xx == 0)
    def _():
        for b in range(blocks):
            load(b).start()

    hl[...] = jnp.zeros_like(hl)
    held = (rhs, h_rhs, h_cols, h_coef, h_inv, c_prev, c_next)
    fetch = [pltpu.make_async_copy(a, b, psem.at[i]) for i, (a, b) in enumerate(zip(smalls, held))]
    for one in fetch:
        one.start()

    barrier = pltpu.get_barrier_semaphore()

    def greet(device):
        pl.semaphore_signal(barrier, inc=1, device_id=device, device_id_type=MESH)

    greet(mate)
    greet(over)
    for step in range(1, NZ):
        greet({"tm": lax.rem(z + step, NZ)})
    middle = (f == 1) | (f == 2)
    up = (f == 3) & (z < NZ - 1)
    down = (f == 0) & (z > 0)

    @pl.when(middle)
    def _():
        greet({"factor": 3 - f})

    @pl.when(up)
    def _():
        greet({"tm": z + 1, "factor": 0})

    @pl.when(down)
    def _():
        greet({"tm": z - 1, "factor": 3})

    pl.semaphore_wait(barrier, NZ + 1 + jnp.where(middle | up | down, 1, 0))

    fetch[0].wait()

    @pl.when(z == 0)
    def _():
        for to in range(1, NZ):
            r_z(to).start()
        rs[...] = rhs[0:8, :]

    def x_send_next(n):
        xcopy(x_block(n - X_OPEN)).wait_send()
        xcopy(x_block(n)).start()

    def x_send_now(n):
        xcopy(x_block(n)).start()

    @pl.when(xx == 0)
    def _():
        load(0).wait()

        @pl.when(z == 0)
        def _():
            for to in range(NZ - 1, 0, -1):
                d_z(to).start()
            dp[p] = cr[p, 0]
            d_x().start()
            d_m(p).start()

        for c in range(nc):
            if c > 0:
                load(2 * c).wait()
            load(2 * c + 1).wait()
            if c < X_OPEN:
                x_send_now(c)
            mcopy(p, 2 * c).start()
            mcopy(p, 2 * c + 1).start()
        for c in range(nc):
            mcopy(q, 2 * c).wait_recv()
            mcopy(q, 2 * c + 1).wait_recv()

    @pl.when((xx == 0) & (z == 0))
    def _():
        for to in range(NZ - 1, 0, -1):
            d_z(to).wait_send()

    def service(n):
        if X_OPEN <= n < nc and n != 3:
            x_send(n)
        if n in (nc, nc + 2):
            for later in range(nc // 2):
                x_send(nc + (n - nc) // 2 * (nc // 2) + later)
        if n < nc:
            x1(n)
        z_send(n)

    service(0)
    service(1)
    for t in range(NZ * nc):
        tile_in(t).start()
    service(2)

    @pl.when(xx == 0)
    def _():
        x_send_next(3)

    @pl.when((xx == 0) & (z > 0))
    def _():
        d_z(1).wait_recv()
        d_x().start()
        d_m(p).start()

    @pl.when(xx == 1)
    def _():
        d_x().wait_recv()
        d_m(p).start()

    d_m(q).wait_recv()

    service(3)
    top = chol_inverse(dp[0, 0:W, :], {3: lambda: service(4), 10: lambda: service(5)})

    service(6)
    side = across(dp[0, W:, :], top)
    low = chol_inverse(
        dp[1, W:, :] - across(side, side), {4: lambda: service(7), 11: lambda: service(8)})
    mixed = -matmul(low, matmul(side, top))
    service(9)
    inv_ref[:W, :W] = top
    inv_ref[:W, W:] = jnp.zeros((W, W), jnp.float32)
    inv_ref[W:, :W] = mixed
    inv_ref[W:, W:] = low

    @pl.when(z > 0)
    def _():
        r_z(1).wait_recv()

    for one in fetch[1:]:
        one.wait()
    seg = jnp.concatenate([rs[0:1, :], rs[1:2, :]], axis=1)
    link = across(jnp.broadcast_to(seg, (8, 2 * W)), inv_ref[...])
    hot = (lax.broadcasted_iota(jnp.int32, (2 * W, 2 * W), 0) == h_cols[...]).astype(jnp.float32)
    target = h_rhs[...] - h_coef[...] * matmul(link, hot)

    def solve(k, want):
        hx[k] = across(want, h_inv[0])
        if k < SWEEPS:
            @pl.when(has_prev)
            def _():
                h_prev(k).start()

            @pl.when(has_next)
            def _():
                h_next(k).start()

    def sweep(k):
        @pl.when(has_prev)
        def _():
            h_next(k).wait_recv()

        @pl.when(has_next)
        def _():
            h_prev(k).wait_recv()

        before = hl[k, 0]
        after = hl[k, 1]
        coupling = before[:, 2 * W - 2:2 * W - 1] * c_prev[0, 0:1, :]
        coupling = coupling + before[:, 2 * W - 1:2 * W] * c_prev[0, 1:2, :]
        coupling = coupling + after[:, 0:1] * c_next[0, 0:1, :]
        coupling = coupling + after[:, 1:2] * c_next[0, 1:2, :]
        solve(k + 1, target - coupling)

    solve(0, target)

    def frow(b):
        fr_ = across(cr[0, b], inv_ref[:, :W]) + across(cr[1, b], inv_ref[:, W:])
        if not isinstance(b, int) or b == 0:
            row = lax.broadcasted_iota(jnp.int32, fr_.shape, 0) + (z * blocks + b) * 2 * W
            depth = lax.broadcasted_iota(jnp.int32, fr_.shape, 1)
            fr_ = jnp.where((row < W) & (depth >= W), 0.0, fr_)
        high, rest = split(fr_)
        at = pl.ds(b * 2 * W, 2 * W)
        left[at, :2 * W] = high
        left[at, 2 * W:] = rest
        gone = across(link, fr_)
        trail[pl.ds(2 * b, 1), :] = rhs[pl.ds(2 * b, 1), :] - gone[0:1, :W]
        trail[pl.ds(2 * b + 1, 1), :] = rhs[pl.ds(2 * b + 1, 1), :] - gone[0:1, W:]

    def fcol(quarter, j):
        gg = across(inv_ref[:, :W], cc[0, quarter, j]) + across(inv_ref[:, W:], cc[1, quarter, j])
        limit = jnp.where((quarter == 0) & (j == 0) & (f == 0), W, 0)
        depth = lax.broadcasted_iota(jnp.int32, gg.shape, 0)
        col = lax.broadcasted_iota(jnp.int32, gg.shape, 1)
        high, rest = split(jnp.where((depth >= W) & (col < limit), 0.0, gg))
        at = quarter * pairs + j
        g[at, :2 * W, :] = high
        g[at, 2 * W:, :] = rest

    def received(n):
        step, j = n // pairs, n % pairs
        take(2 * n)
        take(2 * n + 1)

        @pl.when(z > step)
        def _():
            fcol(z - 1 - step, j)

        @pl.when(z < NZ - 1 - step)
        def _():
            fcol(z + 1 + step, j)

    def early(half):
        half_update(s, left, g, z - 1, 0, EARLY, half, pairs, blocks, range(NZ - 1))
        half_update(s, left, g, z + 1, 0, EARLY, half, pairs, blocks, range(1, NZ))

    for c in range(nc):
        frow(2 * c + 1)
        if c % 3 == 2:
            service(10 + c // 3)
    sweep(0)
    for c in range(nc):
        own_copy(c).wait()
    for t in range(NZ * nc):
        tile_in(t).wait()
    for j in range(pairs):
        fcol(z, j)
    half_update(s, left, g, z, 0, pairs, 1, pairs, blocks, range(NZ))
    service(12)
    for n in range(EARLY):
        received(n)
    early(1)
    service(13)
    sweep(1)
    for c in range(nc):
        x0(c)
        frow(2 * c)
        if c % 3 == 2:
            service(14 + c // 3)
    half_update(s, left, g, z, 0, pairs, 0, pairs, blocks, range(NZ))
    service(16)
    early(0)
    for n in range(17, total):
        service(n)
    hour[...] = hx[SWEEPS, 0:1, :]
    for n in range(EARLY, total // 2):
        received(n)

    for b in range(blocks):
        mcopy(p, b).wait_send()

    @pl.when(xx == 0)
    def _():
        for n in range(nc - X_OPEN, 2 * nc):
            xcopy(x_block(n)).wait_send()

    for m in range(total):
        step, later = m // nc, (m + Z_OPEN) // nc
        if later > step:
            @pl.when((z < NZ - 1) & (z >= step) & (z < later))
            def _():
                fwd(m).wait_send()

            @pl.when((z > 0) & (NZ - 1 - z >= step) & (NZ - 1 - z < later))
            def _():
                bwd(m).wait_send()

    d_m(p).wait_send()

    @pl.when(xx == 0)
    def _():
        d_x().wait_send()

    @pl.when(z == 0)
    def _():
        for to in range(1, NZ):
            r_z(to).wait_send()

    for k in range(SWEEPS):
        @pl.when(has_prev)
        def _():
            h_prev(k).wait_send()

        @pl.when(has_next)
        def _():
            h_next(k).wait_send()


def finish_kernel(nc, s0, s1, s2, s3, left, g, trail, hour, out, trail_out, hour_out, sem):
    s = (s0, s1, s2, s3)
    z = lax.axis_index("tm")
    pairs = nc // 2

    def put(q, j):
        for t in (2 * j, 2 * j + 1):
            pltpu.make_async_copy(s[q].at[t], out.at[:, q * nc + t, 0, :], sem.at[q * nc + t]).start()

    def ready(q, j):
        fore = (z - 1 - q) * pairs + j
        back = (q - z - 1) * pairs + j
        return (z == q) | ((z > q) & (fore < EARLY)) | ((z < q) & (back < EARLY))

    for q in range(NZ):
        for j in range(pairs):
            @pl.when(ready(q, j))
            def _():
                put(q, j)

    trail_out[...] = trail[...]
    hour_out[...] = hour[...]
    for q in range(NZ):
        for j in range(pairs):
            @pl.when(jnp.logical_not(ready(q, j)))
            def _():
                def body(b, carry):
                    at = pl.ds(pl.multiple_of(b * 2 * W, 2 * W), 2 * W)
                    u = product(left[at, :], g[q * pairs + j])
                    s[q][2 * j, at, :] -= u[:, :W]
                    s[q][2 * j + 1, at, :] -= u[:, W:]
                    return carry
                lax.fori_loop(0, 2 * nc, body, 0, unroll=2 * nc)
                put(q, j)

    for q in range(NZ):
        for t in range(nc):
            pltpu.make_async_copy(s[q].at[t], out.at[:, q * nc + t, 0, :], sem.at[q * nc + t]).wait()


def eliminate(schur, link_rhs, hour_rhs, link_cols, link_coef, hour_inverse, couple_prev, couple_next):
    rows_here, tiles, _, w = schur.shape
    nc = tiles // NZ
    pairs = tiles // 2
    total = (NZ - 1) * nc
    dma = pltpu.SemaphoreType.DMA
    f32, bf16 = jnp.float32, jnp.bfloat16
    vmem = pl.BlockSpec(memory_space=pltpu.VMEM)
    hbm = pl.BlockSpec(memory_space=pl.ANY)
    smalls = (link_rhs.reshape(rows_here // w, w), hour_rhs, link_cols, link_coef, hour_inverse,
              couple_prev, couple_next)
    made = pl.pallas_call(
        functools.partial(panel_kernel, nc),
        out_shape=tuple(pltpu.VMEM((nc, rows_here, w), f32) for _ in range(NZ)) + (
            pltpu.VMEM((rows_here, 4 * w), bf16),
            pltpu.VMEM((pairs, 4 * w, 2 * w), bf16),
            pltpu.VMEM((rows_here // w, w), f32),
            pltpu.VMEM((1, 2 * w), f32),
        ),
        in_specs=[pl.BlockSpec(memory_space=pltpu.HBM)] * 8,
        out_specs=(vmem,) * (NZ + 4),
        scratch_shapes=[pltpu.VMEM(a.shape, a.dtype) for a in smalls] + [
            pltpu.VMEM((2, 2 * nc, 2 * w, w), f32),
            pltpu.VMEM((2, NZ, nc // 2, 2 * w, w), f32),
            pltpu.VMEM((2, 2 * w, w), f32),
            pltpu.VMEM((8, w), f32),
            pltpu.VMEM((SWEEPS + 1, 8, 2 * w), f32),
            pltpu.VMEM((SWEEPS, 2, 8, 2 * w), f32),
            pltpu.VMEM((2 * w, 2 * w), f32),
            dma((7,)), dma((2 * nc,)), dma((tiles,)), dma((nc,)),
            dma((2 * nc,)), dma((2 * nc,)), dma((2 * nc,)), dma((2 * nc,)),
            dma((total,)), dma((total,)), dma((total,)), dma((total,)),
            dma((NZ - 1,)), dma, dma, dma, dma, dma, dma((NZ - 1,)), dma,
            dma((SWEEPS, 2)), dma((SWEEPS, 2)),
        ],
        compiler_params=pltpu.CompilerParams(
            collective_id=0, has_side_effects=True, vmem_limit_bytes=12 * 1024 * 1024),
    )(schur, *smalls)
    out, trail, hour = pl.pallas_call(
        functools.partial(finish_kernel, nc),
        out_shape=(
            jax.ShapeDtypeStruct(schur.shape, f32),
            jax.ShapeDtypeStruct((rows_here // w, w), f32),
            jax.ShapeDtypeStruct((1, 2 * w), f32),
        ),
        in_specs=[vmem] * (NZ + 4),
        out_specs=(hbm, vmem, vmem),
        scratch_shapes=[dma((tiles,))],
        compiler_params=pltpu.CompilerParams(vmem_limit_bytes=4 * 1024 * 1024),
    )(*made)
    return out, trail.reshape(-1), hour


def panels_by_step(schur_now, rhs_now):
    rows_here = schur_now.shape[0]
    tiles_here = schur_now.shape[1]
    width = schur_now.shape[3]
    factors = lax.axis_size("factor")
    row_start = lax.axis_index("tm") * rows_here
    global_rows = row_start + jnp.arange(rows_here, dtype=jnp.int32)
    factor_here = lax.axis_index("factor")
    solved = []
    for panel_id in range(PANELS):
        column_tile = panel_id // factors
        owner_index = panel_id % factors
        own_cols = schur_now[:, column_tile, 0, :]
        panel_cols = spread(own_cols, "factor", owner_index)
        panel_first = panel_id * width
        picker = (
            global_rows[:, None] - panel_first == jnp.arange(width, dtype=jnp.int32)[None, :]
        ).astype(jnp.float32)
        block_part = jnp.dot(picker.T, panel_cols, precision=lax.Precision.HIGHEST)
        rhs_part = jnp.dot(picker.T, rhs_now, precision=lax.Precision.HIGHEST)
        diag_block, rhs_segment = lax.psum((block_part, rhs_part), "tm")
        lower_block = jnp.linalg.cholesky(diag_block)
        factor_rows = jax.scipy.linalg.solve_triangular(lower_block, panel_cols.T, lower=True).T
        factor_rows = jnp.where(
            (global_rows < panel_first)[:, None], jnp.zeros_like(factor_rows), factor_rows
        )
        all_factor = lax.all_gather(factor_rows, "tm", axis=0, tiled=True)
        grouped = all_factor.reshape(tiles_here, factors, width, width)
        my_tiles = lax.dynamic_index_in_dim(grouped, factor_here, 1, keepdims=False)
        link_step = jax.scipy.linalg.solve_triangular(lower_block, rhs_segment, lower=True)
        rhs_now = rhs_now - jnp.dot(factor_rows, link_step, precision=lax.Precision.HIGHEST)
        update = jnp.einsum("rk,tck->rtc", factor_rows, my_tiles, precision=lax.Precision.HIGHEST)
        schur_now = schur_now - update[:, :, None, :]
        solved.append(link_step)
    return schur_now, rhs_now, jnp.concatenate(solved)


def shards(
    schur_matrix, link_rhs, hour_rhs, link_cols, link_coef, hour_inverse, couple_prev, couple_next
):
    rows_here, tiles, _, width = schur_matrix.shape
    zs = lax.axis_size("tm")
    fused = lax.axis_size("factor") == 4 and zs == 4 and width == 128 and hour_rhs.shape == (1, 256)
    fused = fused and tiles % (2 * zs) == 0 and rows_here * zs == tiles * 4 * width and rows_here <= 3072
    if fused:
        return eliminate(
            schur_matrix, link_rhs, hour_rhs, link_cols, link_coef, hour_inverse, couple_prev, couple_next)
    schur_now, rhs_now, link_values = panels_by_step(schur_matrix, link_rhs)
    one_hot = (
        link_cols[:, :, None] == jnp.arange(PANELS * width, dtype=jnp.int32)[None, None, :]
    ).astype(jnp.float32)
    looked = jnp.einsum("hik,k->hi", one_hot, link_values, precision=lax.Precision.HIGHEST)
    target = hour_rhs - link_coef * looked
    hour_state = jnp.einsum("hik,hk->hi", hour_inverse, target, precision=lax.Precision.HIGHEST)
    for sweep_id in range(SWEEPS):
        border_pairs = jnp.concatenate((hour_state[:, :BW], hour_state[:, -BW:]), axis=1)
        padded = with_halo(border_pairs, ((("tm", "factor"), 0),), 1)
        prev_last = padded[:-2, BW:]
        next_first = padded[2:, :BW]
        coupling = jnp.einsum("hbi,hb->hi", couple_prev, prev_last, precision=lax.Precision.HIGHEST)
        coupling = coupling + jnp.einsum(
            "hbi,hb->hi", couple_next, next_first, precision=lax.Precision.HIGHEST
        )
        hour_state = jnp.einsum(
            "hik,hk->hi", hour_inverse, target - coupling, precision=lax.Precision.HIGHEST
        )
    return (schur_now, rhs_now, hour_state)


def solution(mesh):
    placed = (
        P(("parts", "tm"), None, "factor", None),
        P(("parts", "tm")),
        P(("parts", "tm", "factor"), None),
        P(("parts", "tm", "factor"), None),
        P(("parts", "tm", "factor"), None),
        P(("parts", "tm", "factor"), None, None),
        P(("parts", "tm", "factor"), None, None),
        P(("parts", "tm", "factor"), None, None),
    )
    return jax.shard_map(
        shards,
        mesh=mesh,
        in_specs=placed,
        out_specs=(
            P(("parts", "tm"), None, "factor", None),
            P(("parts", "tm")),
            P(("parts", "tm", "factor"), None),
        ),
        check_vma=False,
    )
```

```python
import functools

import jax
import jax.numpy as jnp
from jax import lax
from jax.experimental import pallas as pl
from jax.experimental.pallas import tpu as pltpu
from jax.sharding import PartitionSpec as P

PANELS = 2
BW = 2
SWEEPS = 2
HIGH = lax.Precision.HIGHEST
MESH = pl.DeviceIdType.MESH


def spread(array, axis, root):
    mine = lax.axis_index(axis) == root
    return lax.psum(jnp.where(mine, array, jnp.zeros_like(array)), axis)


def with_halo(cells, sides, width):
    for axis, dim in sides:
        count = lax.axis_size(axis)
        ends = count - 1
        head = lax.slice_in_dim(cells, 0, width, axis=dim)
        tail = lax.slice_in_dim(cells, cells.shape[dim] - width, cells.shape[dim], axis=dim)
        cells = jnp.concatenate(
            [
                lax.ppermute(tail, axis, [(i, (i + 1) % count) for i in range(ends)]),
                cells,
                lax.ppermute(head, axis, [((i + 1) % count, i) for i in range(ends)]),
            ],
            axis=dim,
        )
    return cells


W = 128
NZ = 4
Z_OPEN = 5
X_OPEN = 2
EARLY = 2


def across(a, b):
    return lax.dot_general(
        a, b, (((1,), (1,)), ((), ())), precision=HIGH, preferred_element_type=jnp.float32)


def matmul(a, b):
    return jnp.dot(a, b, precision=HIGH, preferred_element_type=jnp.float32)


def split(a):
    high = a.astype(jnp.bfloat16)
    return high, (a - high.astype(jnp.float32)).astype(jnp.bfloat16)


def chol_inverse(block, hooks):
    count = W // 8
    rows = [block[8 * i:8 * i + 8, :] for i in range(count)]
    lane = lax.broadcasted_iota(jnp.int32, (8, W), 1)
    sub = lax.broadcasted_iota(jnp.int32, (8, W), 0)
    for b in range(count):
        j0 = 8 * b
        here = (lane >= j0) & (lane < j0 + 8)
        p = rows[b]
        piv = [jnp.broadcast_to(p[:, j0 + t:j0 + t + 1], (8, W)) for t in range(8)]
        p = jnp.where(here, jnp.where(lane - j0 == sub, 1.0, 0.0), p)
        done = p
        for t in range(8):
            d = piv[t][t:t + 1, :]
            r = p[t:t + 1, :]
            done = jnp.where(sub == t, r * lax.rsqrt(d), done)
            inv = 1.0 / d
            rr = r * inv
            p = jnp.where(sub == t, rr, p - piv[t] * rr)
            for u in range(t + 1, 8):
                bu = piv[u][t:t + 1, :] * inv
                piv[u] = jnp.where(sub == t, bu, piv[u] - piv[t] * bu)
        for i in range(b + 1, count):
            old = rows[i]
            now = jnp.where(here, 0.0, old)
            for t in range(8):
                now = now - old[:, j0 + t:j0 + t + 1] * p[t:t + 1, :]
            rows[i] = now
        rows[b] = done
        if b in hooks:
            hooks[b]()
    full = jnp.concatenate(rows, axis=0)
    low = lax.broadcasted_iota(jnp.int32, (W, W), 0) >= lax.broadcasted_iota(jnp.int32, (W, W), 1)
    return jnp.where(low, full, 0.0)


def product(left, right):
    high = left[:, :2 * W]
    rows = jnp.concatenate([high, high, left[:, 2 * W:]], axis=1)
    first = right[:2 * W, :]
    cols = jnp.concatenate([first, right[2 * W:, :], first], axis=0)
    return jnp.dot(rows, cols, preferred_element_type=jnp.float32)


def half_update(s, left, g, q, first, last, half, pairs, blocks, among):
    for qq in among:
        @pl.when(q == qq)
        def _():
            @pl.loop(first, last)
            def _(j):
                right = g.at[qq * pairs + j]

                def body(b, carry):
                    at = pl.ds(pl.multiple_of((2 * b + half) * 2 * W, 2 * W), 2 * W)
                    u = product(left[at, :], right[...])
                    s[qq][2 * j, at, :] -= u[:, :W]
                    s[qq][2 * j + 1, at, :] -= u[:, W:]
                    return carry
                lax.fori_loop(0, blocks // 2, body, 0, unroll=blocks // 2)


def panel_kernel(nc, s_hbm, *refs):
    smalls, refs = refs[:7], refs[7:]
    panel_body(nc, s_hbm, smalls, *refs)


def panel_body(
    nc, s_hbm, smalls,
    s0, s1, s2, s3, left, g, trail, hour,
    rhs, h_rhs, h_cols, h_coef, h_inv, c_prev, c_next, cr, cc, dp, rs, hx, hl, inv_ref,
    psem, lsem, ssem, osem, xs, xr, ms, mr, fs, fr, bs, br, dzs, dzr, dxs, dxr, dms, dmr, rss, rsr, hs, hr,
):
    s = (s0, s1, s2, s3)
    f = lax.axis_index("factor")
    z = lax.axis_index("tm")
    p = lax.rem(f, 2)
    q = 1 - p
    xx = lax.div(f, 2)
    mate = {"factor": f + 1 - 2 * p}
    over = {"factor": f + 2 - 4 * xx}
    blocks = 2 * nc
    pairs = nc // 2

    def remote(src, dst, send, recv, device):
        return pltpu.make_async_remote_copy(
            src_ref=src, dst_ref=dst, send_sem=send, recv_sem=recv, device_id=device, device_id_type=MESH)

    def load(b):
        return pltpu.make_async_copy(
            s_hbm.at[b * 2 * W:(b + 1) * 2 * W, 0, 0, :], cr.at[p, b], lsem.at[b])

    def tile_in(t):
        return pltpu.make_async_copy(s_hbm.at[:, t, 0, :], s[t // nc].at[t % nc], ssem.at[t])

    def xcopy(b):
        return remote(cr.at[p, b], cr.at[p, b], xs.at[b], xr.at[b], over)

    def mcopy(panel, b):
        return remote(cr.at[panel, b], cr.at[panel, b], ms.at[b], mr.at[b], mate)

    def slot(quarter, c):
        return cc.at[:, quarter, c // 2, (c % 2) * W:(c % 2 + 1) * W]

    def mine(c):
        return cr.at[:, 2 * c + xx, pl.ds(pl.multiple_of(p * W, W), W)]

    def own_copy(c):
        return pltpu.make_async_copy(mine(c), slot(z, c), osem.at[c])

    def fwd(m):
        c = m % nc
        where = slot(z - m // nc, c)
        return remote(mine(c) if m < nc else where, where, fs.at[m], fr.at[m], {"tm": z + 1})

    def bwd(m):
        c = m % nc
        where = slot(z + m // nc, c)
        return remote(mine(c) if m < nc else where, where, bs.at[m], br.at[m], {"tm": z - 1})

    def fwd_in(m):
        where = slot(z - 1 - m // nc, m % nc)
        return remote(where, where, fs.at[m], fr.at[m], {"tm": z - 1})

    def bwd_in(m):
        where = slot(z + 1 + m // nc, m % nc)
        return remote(where, where, bs.at[m], br.at[m], {"tm": z + 1})

    total = (NZ - 1) * nc

    def z_send(m):
        if not 0 <= m < total:
            return
        step = m // nc
        if step == 0:
            own_copy(m).start()

        @pl.when((z < NZ - 1) & (z >= step))
        def _():
            if step > 0:
                fwd_in(m - nc).wait_recv()
            if m >= Z_OPEN:
                fwd(m - Z_OPEN).wait_send()
            fwd(m).start()

        @pl.when((z > 0) & (NZ - 1 - z >= step))
        def _():
            if step > 0:
                bwd_in(m - nc).wait_recv()
            if m >= Z_OPEN:
                bwd(m - Z_OPEN).wait_send()
            bwd(m).start()

    def take(m):
        @pl.when(z == NZ - 1)
        def _():
            fwd_in(m).wait_recv()

        @pl.when(z == 0)
        def _():
            bwd_in(m).wait_recv()

    def x_block(n):
        return 2 * n + 1 if n < nc else 2 * (n - nc)

    def x_send(n):
        if n < 2 * nc:
            @pl.when(xx == 0)
            def _():
                if X_OPEN <= n < nc:
                    xcopy(x_block(n - X_OPEN)).wait_send()
                xcopy(x_block(n)).start()

    def x1(c):
        @pl.when(xx == 1)
        def _():
            xcopy(2 * c + 1).wait_recv()
            mcopy(p, 2 * c + 1).start()
            mcopy(q, 2 * c + 1).wait_recv()

    def x0(c):
        @pl.when(xx == 1)
        def _():
            xcopy(2 * c).wait_recv()
            mcopy(p, 2 * c).start()
            mcopy(q, 2 * c).wait_recv()

    def d_z(to):
        return remote(dp.at[p], dp.at[p], dzs.at[to - 1], dzr, {"tm": to})

    def r_z(to):
        return remote(rhs.at[0:8], rs, rss.at[to - 1], rsr, {"tm": to})

    def d_x():
        return remote(dp.at[p], dp.at[p], dxs, dxr, over)

    def d_m(panel):
        return remote(dp.at[panel], dp.at[panel], dms, dmr, mate)

    has_prev = (z > 0) | (f > 0)
    has_next = (z < NZ - 1) | (f < 3)

    def h_prev(k):
        return remote(hx.at[k], hl.at[k, 1], hs.at[k, 0], hr.at[k, 1],
                      {"tm": jnp.where(f > 0, z, z - 1), "factor": jnp.where(f > 0, f - 1, 3)})

    def h_next(k):
        return remote(hx.at[k], hl.at[k, 0], hs.at[k, 1], hr.at[k, 0],
                      {"tm": jnp.where(f < 3, z, z + 1), "factor": jnp.where(f < 3, f + 1, 0)})

    @pl.when(xx == 0)
    def _():
        for b in range(blocks):
            load(b).start()

    hl[...] = jnp.zeros_like(hl)
    held = (rhs, h_rhs, h_cols, h_coef, h_inv, c_prev, c_next)
    fetch = [pltpu.make_async_copy(a, b, psem.at[i]) for i, (a, b) in enumerate(zip(smalls, held))]
    for one in fetch:
        one.start()

    barrier = pltpu.get_barrier_semaphore()

    def greet(device):
        pl.semaphore_signal(barrier, inc=1, device_id=device, device_id_type=MESH)

    greet(mate)
    greet(over)
    for step in range(1, NZ):
        greet({"tm": lax.rem(z + step, NZ)})
    middle = (f == 1) | (f == 2)
    up = (f == 3) & (z < NZ - 1)
    down = (f == 0) & (z > 0)

    @pl.when(middle)
    def _():
        greet({"factor": 3 - f})

    @pl.when(up)
    def _():
        greet({"tm": z + 1, "factor": 0})

    @pl.when(down)
    def _():
        greet({"tm": z - 1, "factor": 3})

    pl.semaphore_wait(barrier, NZ + 1 + jnp.where(middle | up | down, 1, 0))

    fetch[0].wait()

    @pl.when(z == 0)
    def _():
        for to in range(1, NZ):
            r_z(to).start()
        rs[...] = rhs[0:8, :]

    def x_send_next(n):
        xcopy(x_block(n - X_OPEN)).wait_send()
        xcopy(x_block(n)).start()

    def x_send_now(n):
        xcopy(x_block(n)).start()

    @pl.when(xx == 0)
    def _():
        load(0).wait()

        @pl.when(z == 0)
        def _():
            dp[p] = cr[p, 0]
            d_x().start()
            for to in range(NZ - 1, 0, -1):
                d_z(to).start()
            d_m(p).start()

        for c in range(nc):
            if c > 0:
                load(2 * c).wait()
            load(2 * c + 1).wait()
            if c < X_OPEN:
                x_send_now(c)
            mcopy(p, 2 * c).start()
            mcopy(p, 2 * c + 1).start()
        for c in range(nc):
            mcopy(q, 2 * c).wait_recv()
            mcopy(q, 2 * c + 1).wait_recv()

    @pl.when((xx == 1) & (z == 0))
    def _():
        d_x().wait_recv()
        for to in range(NZ - 1, 0, -1):
            d_z(to).start()
        d_m(p).start()

    @pl.when(z == 0)
    def _():
        for to in range(NZ - 1, 0, -1):
            d_z(to).wait_send()

    def service(n):
        if X_OPEN <= n < nc and n != 3:
            x_send(n)
        if n in (nc, nc + 2):
            for later in range(nc // 2):
                x_send(nc + (n - nc) // 2 * (nc // 2) + later)
        if n < nc:
            x1(n)
        z_send(n)

    service(0)
    service(1)
    for t in range(NZ * nc):
        tile_in(t).start()
    service(2)

    @pl.when(xx == 0)
    def _():
        x_send_next(3)

    @pl.when(z > 0)
    def _():
        d_z(1).wait_recv()
        d_m(p).start()

    d_m(q).wait_recv()

    service(3)
    top = chol_inverse(dp[0, 0:W, :], {3: lambda: service(4), 10: lambda: service(5)})

    service(6)
    side = across(dp[0, W:, :], top)
    low = chol_inverse(
        dp[1, W:, :] - across(side, side), {4: lambda: service(7), 11: lambda: service(8)})
    mixed = -matmul(low, matmul(side, top))
    service(9)
    inv_ref[:W, :W] = top
    inv_ref[:W, W:] = jnp.zeros((W, W), jnp.float32)
    inv_ref[W:, :W] = mixed
    inv_ref[W:, W:] = low

    @pl.when(z > 0)
    def _():
        r_z(1).wait_recv()

    for one in fetch[1:]:
        one.wait()
    seg = jnp.concatenate([rs[0:1, :], rs[1:2, :]], axis=1)
    link = across(jnp.broadcast_to(seg, (8, 2 * W)), inv_ref[...])
    hot = (lax.broadcasted_iota(jnp.int32, (2 * W, 2 * W), 0) == h_cols[...]).astype(jnp.float32)
    target = h_rhs[...] - h_coef[...] * matmul(link, hot)

    def solve(k, want):
        hx[k] = across(want, h_inv[0])
        if k < SWEEPS:
            @pl.when(has_prev)
            def _():
                h_prev(k).start()

            @pl.when(has_next)
            def _():
                h_next(k).start()

    def sweep(k):
        @pl.when(has_prev)
        def _():
            h_next(k).wait_recv()

        @pl.when(has_next)
        def _():
            h_prev(k).wait_recv()

        before = hl[k, 0]
        after = hl[k, 1]
        coupling = before[:, 2 * W - 2:2 * W - 1] * c_prev[0, 0:1, :]
        coupling = coupling + before[:, 2 * W - 1:2 * W] * c_prev[0, 1:2, :]
        coupling = coupling + after[:, 0:1] * c_next[0, 0:1, :]
        coupling = coupling + after[:, 1:2] * c_next[0, 1:2, :]
        solve(k + 1, target - coupling)

    solve(0, target)

    def frow(b):
        fr_ = across(cr[0, b], inv_ref[:, :W]) + across(cr[1, b], inv_ref[:, W:])
        if not isinstance(b, int) or b == 0:
            row = lax.broadcasted_iota(jnp.int32, fr_.shape, 0) + (z * blocks + b) * 2 * W
            depth = lax.broadcasted_iota(jnp.int32, fr_.shape, 1)
            fr_ = jnp.where((row < W) & (depth >= W), 0.0, fr_)
        high, rest = split(fr_)
        at = pl.ds(b * 2 * W, 2 * W)
        left[at, :2 * W] = high
        left[at, 2 * W:] = rest
        gone = across(link, fr_)
        trail[pl.ds(2 * b, 1), :] = rhs[pl.ds(2 * b, 1), :] - gone[0:1, :W]
        trail[pl.ds(2 * b + 1, 1), :] = rhs[pl.ds(2 * b + 1, 1), :] - gone[0:1, W:]

    def fcol(quarter, j):
        gg = across(inv_ref[:, :W], cc[0, quarter, j]) + across(inv_ref[:, W:], cc[1, quarter, j])
        limit = jnp.where((quarter == 0) & (j == 0) & (f == 0), W, 0)
        depth = lax.broadcasted_iota(jnp.int32, gg.shape, 0)
        col = lax.broadcasted_iota(jnp.int32, gg.shape, 1)
        high, rest = split(jnp.where((depth >= W) & (col < limit), 0.0, gg))
        at = quarter * pairs + j
        g[at, :2 * W, :] = high
        g[at, 2 * W:, :] = rest

    def received(n):
        step, j = n // pairs, n % pairs
        take(2 * n)
        take(2 * n + 1)

        @pl.when(z > step)
        def _():
            fcol(z - 1 - step, j)

        @pl.when(z < NZ - 1 - step)
        def _():
            fcol(z + 1 + step, j)

    def early(half):
        half_update(s, left, g, z - 1, 0, EARLY, half, pairs, blocks, range(NZ - 1))
        half_update(s, left, g, z + 1, 0, EARLY, half, pairs, blocks, range(1, NZ))

    for c in range(nc):
        frow(2 * c + 1)
        if c % 3 == 2:
            service(10 + c // 3)
    sweep(0)
    for c in range(nc):
        own_copy(c).wait()
    for t in range(NZ * nc):
        tile_in(t).wait()
    for j in range(pairs):
        fcol(z, j)
    half_update(s, left, g, z, 0, pairs, 1, pairs, blocks, range(NZ))
    service(12)
    for n in range(EARLY):
        received(n)
    early(1)
    service(13)
    sweep(1)
    for c in range(nc):
        x0(c)
        frow(2 * c)
        if c % 3 == 2:
            service(14 + c // 3)
    half_update(s, left, g, z, 0, pairs, 0, pairs, blocks, range(NZ))
    service(16)
    early(0)
    for n in range(17, total):
        service(n)
    hour[...] = hx[SWEEPS, 0:1, :]
    for n in range(EARLY, total // 2):
        received(n)

    for b in range(blocks):
        mcopy(p, b).wait_send()

    @pl.when(xx == 0)
    def _():
        for n in range(nc - X_OPEN, 2 * nc):
            xcopy(x_block(n)).wait_send()

    for m in range(total):
        step, later = m // nc, (m + Z_OPEN) // nc
        if later > step:
            @pl.when((z < NZ - 1) & (z >= step) & (z < later))
            def _():
                fwd(m).wait_send()

            @pl.when((z > 0) & (NZ - 1 - z >= step) & (NZ - 1 - z < later))
            def _():
                bwd(m).wait_send()

    d_m(p).wait_send()

    @pl.when((xx == 0) & (z == 0))
    def _():
        d_x().wait_send()

    @pl.when(z == 0)
    def _():
        for to in range(1, NZ):
            r_z(to).wait_send()

    for k in range(SWEEPS):
        @pl.when(has_prev)
        def _():
            h_prev(k).wait_send()

        @pl.when(has_next)
        def _():
            h_next(k).wait_send()


def finish_kernel(nc, s0, s1, s2, s3, left, g, trail, hour, out, trail_out, hour_out, sem):
    s = (s0, s1, s2, s3)
    z = lax.axis_index("tm")
    pairs = nc // 2

    def put(q, j):
        for t in (2 * j, 2 * j + 1):
            pltpu.make_async_copy(s[q].at[t], out.at[:, q * nc + t, 0, :], sem.at[q * nc + t]).start()

    def ready(q, j):
        fore = (z - 1 - q) * pairs + j
        back = (q - z - 1) * pairs + j
        return (z == q) | ((z > q) & (fore < EARLY)) | ((z < q) & (back < EARLY))

    for q in range(NZ):
        for j in range(pairs):
            @pl.when(ready(q, j))
            def _():
                put(q, j)

    trail_out[...] = trail[...]
    hour_out[...] = hour[...]
    for q in range(NZ):
        for j in range(pairs):
            @pl.when(jnp.logical_not(ready(q, j)))
            def _():
                def body(b, carry):
                    at = pl.ds(pl.multiple_of(b * 2 * W, 2 * W), 2 * W)
                    u = product(left[at, :], g[q * pairs + j])
                    s[q][2 * j, at, :] -= u[:, :W]
                    s[q][2 * j + 1, at, :] -= u[:, W:]
                    return carry
                lax.fori_loop(0, 2 * nc, body, 0, unroll=2 * nc)
                put(q, j)

    for q in range(NZ):
        for t in range(nc):
            pltpu.make_async_copy(s[q].at[t], out.at[:, q * nc + t, 0, :], sem.at[q * nc + t]).wait()


def eliminate(schur, link_rhs, hour_rhs, link_cols, link_coef, hour_inverse, couple_prev, couple_next):
    rows_here, tiles, _, w = schur.shape
    nc = tiles // NZ
    pairs = tiles // 2
    total = (NZ - 1) * nc
    dma = pltpu.SemaphoreType.DMA
    f32, bf16 = jnp.float32, jnp.bfloat16
    vmem = pl.BlockSpec(memory_space=pltpu.VMEM)
    hbm = pl.BlockSpec(memory_space=pl.ANY)
    smalls = (link_rhs.reshape(rows_here // w, w), hour_rhs, link_cols, link_coef, hour_inverse,
              couple_prev, couple_next)
    made = pl.pallas_call(
        functools.partial(panel_kernel, nc),
        out_shape=tuple(pltpu.VMEM((nc, rows_here, w), f32) for _ in range(NZ)) + (
            pltpu.VMEM((rows_here, 4 * w), bf16),
            pltpu.VMEM((pairs, 4 * w, 2 * w), bf16),
            pltpu.VMEM((rows_here // w, w), f32),
            pltpu.VMEM((1, 2 * w), f32),
        ),
        in_specs=[pl.BlockSpec(memory_space=pltpu.HBM)] * 8,
        out_specs=(vmem,) * (NZ + 4),
        scratch_shapes=[pltpu.VMEM(a.shape, a.dtype) for a in smalls] + [
            pltpu.VMEM((2, 2 * nc, 2 * w, w), f32),
            pltpu.VMEM((2, NZ, nc // 2, 2 * w, w), f32),
            pltpu.VMEM((2, 2 * w, w), f32),
            pltpu.VMEM((8, w), f32),
            pltpu.VMEM((SWEEPS + 1, 8, 2 * w), f32),
            pltpu.VMEM((SWEEPS, 2, 8, 2 * w), f32),
            pltpu.VMEM((2 * w, 2 * w), f32),
            dma((7,)), dma((2 * nc,)), dma((tiles,)), dma((nc,)),
            dma((2 * nc,)), dma((2 * nc,)), dma((2 * nc,)), dma((2 * nc,)),
            dma((total,)), dma((total,)), dma((total,)), dma((total,)),
            dma((NZ - 1,)), dma, dma, dma, dma, dma, dma((NZ - 1,)), dma,
            dma((SWEEPS, 2)), dma((SWEEPS, 2)),
        ],
        compiler_params=pltpu.CompilerParams(
            collective_id=0, has_side_effects=True, vmem_limit_bytes=12 * 1024 * 1024),
    )(schur, *smalls)
    out, trail, hour = pl.pallas_call(
        functools.partial(finish_kernel, nc),
        out_shape=(
            jax.ShapeDtypeStruct(schur.shape, f32),
            jax.ShapeDtypeStruct((rows_here // w, w), f32),
            jax.ShapeDtypeStruct((1, 2 * w), f32),
        ),
        in_specs=[vmem] * (NZ + 4),
        out_specs=(hbm, vmem, vmem),
        scratch_shapes=[dma((tiles,))],
        compiler_params=pltpu.CompilerParams(vmem_limit_bytes=4 * 1024 * 1024),
    )(*made)
    return out, trail.reshape(-1), hour


def panels_by_step(schur_now, rhs_now):
    rows_here = schur_now.shape[0]
    tiles_here = schur_now.shape[1]
    width = schur_now.shape[3]
    factors = lax.axis_size("factor")
    row_start = lax.axis_index("tm") * rows_here
    global_rows = row_start + jnp.arange(rows_here, dtype=jnp.int32)
    factor_here = lax.axis_index("factor")
    solved = []
    for panel_id in range(PANELS):
        column_tile = panel_id // factors
        owner_index = panel_id % factors
        own_cols = schur_now[:, column_tile, 0, :]
        panel_cols = spread(own_cols, "factor", owner_index)
        panel_first = panel_id * width
        picker = (
            global_rows[:, None] - panel_first == jnp.arange(width, dtype=jnp.int32)[None, :]
        ).astype(jnp.float32)
        block_part = jnp.dot(picker.T, panel_cols, precision=lax.Precision.HIGHEST)
        rhs_part = jnp.dot(picker.T, rhs_now, precision=lax.Precision.HIGHEST)
        diag_block, rhs_segment = lax.psum((block_part, rhs_part), "tm")
        lower_block = jnp.linalg.cholesky(diag_block)
        factor_rows = jax.scipy.linalg.solve_triangular(lower_block, panel_cols.T, lower=True).T
        factor_rows = jnp.where(
            (global_rows < panel_first)[:, None], jnp.zeros_like(factor_rows), factor_rows
        )
        all_factor = lax.all_gather(factor_rows, "tm", axis=0, tiled=True)
        grouped = all_factor.reshape(tiles_here, factors, width, width)
        my_tiles = lax.dynamic_index_in_dim(grouped, factor_here, 1, keepdims=False)
        link_step = jax.scipy.linalg.solve_triangular(lower_block, rhs_segment, lower=True)
        rhs_now = rhs_now - jnp.dot(factor_rows, link_step, precision=lax.Precision.HIGHEST)
        update = jnp.einsum("rk,tck->rtc", factor_rows, my_tiles, precision=lax.Precision.HIGHEST)
        schur_now = schur_now - update[:, :, None, :]
        solved.append(link_step)
    return schur_now, rhs_now, jnp.concatenate(solved)


def shards(
    schur_matrix, link_rhs, hour_rhs, link_cols, link_coef, hour_inverse, couple_prev, couple_next
):
    rows_here, tiles, _, width = schur_matrix.shape
    zs = lax.axis_size("tm")
    fused = lax.axis_size("factor") == 4 and zs == 4 and width == 128 and hour_rhs.shape == (1, 256)
    fused = fused and tiles % (2 * zs) == 0 and rows_here * zs == tiles * 4 * width and rows_here <= 3072
    if fused:
        return eliminate(
            schur_matrix, link_rhs, hour_rhs, link_cols, link_coef, hour_inverse, couple_prev, couple_next)
    schur_now, rhs_now, link_values = panels_by_step(schur_matrix, link_rhs)
    one_hot = (
        link_cols[:, :, None] == jnp.arange(PANELS * width, dtype=jnp.int32)[None, None, :]
    ).astype(jnp.float32)
    looked = jnp.einsum("hik,k->hi", one_hot, link_values, precision=lax.Precision.HIGHEST)
    target = hour_rhs - link_coef * looked
    hour_state = jnp.einsum("hik,hk->hi", hour_inverse, target, precision=lax.Precision.HIGHEST)
    for sweep_id in range(SWEEPS):
        border_pairs = jnp.concatenate((hour_state[:, :BW], hour_state[:, -BW:]), axis=1)
        padded = with_halo(border_pairs, ((("tm", "factor"), 0),), 1)
        prev_last = padded[:-2, BW:]
        next_first = padded[2:, :BW]
        coupling = jnp.einsum("hbi,hb->hi", couple_prev, prev_last, precision=lax.Precision.HIGHEST)
        coupling = coupling + jnp.einsum(
            "hbi,hb->hi", couple_next, next_first, precision=lax.Precision.HIGHEST
        )
        hour_state = jnp.einsum(
            "hik,hk->hi", hour_inverse, target - coupling, precision=lax.Precision.HIGHEST
        )
    return (schur_now, rhs_now, hour_state)


def solution(mesh):
    placed = (
        P(("parts", "tm"), None, "factor", None),
        P(("parts", "tm")),
        P(("parts", "tm", "factor"), None),
        P(("parts", "tm", "factor"), None),
        P(("parts", "tm", "factor"), None),
        P(("parts", "tm", "factor"), None, None),
        P(("parts", "tm", "factor"), None, None),
        P(("parts", "tm", "factor"), None, None),
    )
    return jax.shard_map(
        shards,
        mesh=mesh,
        in_specs=placed,
        out_specs=(
            P(("parts", "tm"), None, "factor", None),
            P(("parts", "tm")),
            P(("parts", "tm", "factor"), None),
        ),
        check_vma=False,
    )
```
